512 devices in a mesh: gz: 16 (over z, core), ga: 32 (over y, x).
Axes of the slice: x: 4, y: 8, z: 8, core: 2. Of those that a mesh axis runs over, the one named last changes fastest.
Arguments:
- right_sides: float32 [16, 32, 32, 512], P('gz', 'ga'), may hold values from -6 to 6
- diag_inverse: float32 [16, 32, 512, 512], P('gz', 'ga'), as said below
- chain_block: float32 [16, 32, 512, 512], P('gz', 'ga')
- top_block: float32 [16, 32, 256, 512], P('gz', 'ga'), may hold values from -0.0234375 to 0.0234375
- top_rows: int32 [16, 32, 256], P('gz', 'ga'), may hold values from 0 to 1023, as said below
- live_cols: int32 [16, 32], P('gz', 'ga'), may hold values from 128 to 512, as said below
- top_right: float32 [32, 1024], replicated, may hold values from -6 to 6
- top_inverse: float32 [1024, 1024], P('ga'), as said below
Outputs:
- solution: float32 [16, 32, 32, 512], P('gz', 'ga')
- top_solution: float32 [32, 1024], replicated
The draws below stay inside these ranges and needn't reach their ends.
Inputs may be any that keep to these rules, and one draw needn't show every extreme that they name: diag_inverse[g,k] and top_inverse are lower triangular. top_inverse is lower triangular. `top_rows`: the 256 entries of one chain supernode are distinct. `live_cols`: every entry is a multiple of 128; the last supernode of every chain (position 15) has all 512 columns live.
All inputs are finite; a program needn't handle non-finite values.
Results may differ from the reference program's by a relative error of at most 0.0003.
Values sent between devices are 32-bit elements; how exact they have to be, the bound alone decides.
No kernel may reach another device: no remote copies, remote signals or barrier semaphores. Data moves between devices by JAX's collectives and lax.ppermute only.
A program may use at most 128 MiB of HBM per device.

```python
import math
import jax
import jax.numpy as jnp
from jax import lax

NRHS = 32
W = 512
TILE = 128
P_SIZE = 256
WT = 1024
BRANCHES = 2
SUBTREE_GROUPS = 16
CHAIN_SPAN = 32
CHAIN = 16
DEVICES = 512


def channel_rates(key, slow_share):
    magnitude_random_key, gradual_random_key, decay_random_key, quick_random_key, spike_random_key = jax.random.split(key, 5)
    array_shape = (SUBTREE_GROUPS, CHAIN_SPAN, W)
    scales = jnp.exp(jax.random.uniform(magnitude_random_key, array_shape, jnp.float32, math.log(0.8), math.log(1.2)))
    gradual_mask = jax.random.uniform(gradual_random_key, array_shape, jnp.float32) < slow_share
    gradual_decay_rates = 0.1 ** (1.0 / CHAIN) * jax.random.uniform(decay_random_key, array_shape, jnp.float32, 0.97, 1.0)
    quick_decay_rates = jax.random.uniform(quick_random_key, array_shape, jnp.float32, 0.2, 0.6)
    spike_mask = jax.random.uniform(spike_random_key, (SUBTREE_GROUPS, CHAIN_SPAN, 1), jnp.float32) < 0.1
    decay_rates = jnp.where(gradual_mask, gradual_decay_rates, quick_decay_rates) * jnp.where(spike_mask, 0.6, 1.0)
    return (scales, decay_rates)


def lower_parts(size):
    row_index = lax.broadcasted_iota(jnp.int32, (size, size), 0)
    col_index = lax.broadcasted_iota(jnp.int32, (size, size), 1)
    return (row_index == col_index, row_index > col_index)


def draw_diag_inverse(key, part):
    slow_share = 0.5
    scales, decay_rates = channel_rates(key, slow_share)
    key = jax.random.fold_in(key, 3)
    noise_draw = jax.random.normal(key, (SUBTREE_GROUPS, CHAIN_SPAN, W, W), jnp.float32)
    on_diag, below_diag = lower_parts(W)
    return jnp.where(on_diag, scales[..., :, None], jnp.where(below_diag, noise_draw * (0.3 / math.sqrt(W)), 0.0))


def draw_chain_block(key, part):
    slow_share = 0.5
    scales, decay_rates = channel_rates(key, slow_share)
    key = jax.random.fold_in(key, 5)
    noise_draw = jax.random.normal(key, (SUBTREE_GROUPS, CHAIN_SPAN, W, W), jnp.float32)
    on_diag, below_diag = lower_parts(W)
    return -(jnp.where(on_diag, (decay_rates / scales)[..., :, None], 0.0) + noise_draw * (0.25 / math.sqrt(W)))


def draw_top_inverse(key, part):
    key = jax.random.fold_in(key, 7)
    magnitude_random_key, noise_key = jax.random.split(key)
    scales = jnp.exp(jax.random.uniform(magnitude_random_key, (WT,), jnp.float32, math.log(0.8), math.log(1.25)))
    noise_draw = jax.random.normal(noise_key, (WT, WT), jnp.float32)
    on_diag, below_diag = lower_parts(WT)
    return jnp.where(on_diag, scales[:, None], jnp.where(below_diag, noise_draw * (0.3 / math.sqrt(WT)), 0.0))


def draw_top_rows(key, part):
    key = jax.random.fold_in(key, 11)
    scores = jax.random.randint(key, (SUBTREE_GROUPS, CHAIN_SPAN, WT), 0, 2 ** 19, jnp.int32) * WT
    scores = scores + lax.broadcasted_iota(jnp.int32, (SUBTREE_GROUPS, CHAIN_SPAN, WT), 2)
    ordering = jnp.argsort(scores, axis=-1, stable=True)
    return ordering[..., :P_SIZE].astype(jnp.int32)


def draw_live_cols(key, part):
    key = jax.random.fold_in(key, 13)
    tile_count = jax.random.randint(key, (SUBTREE_GROUPS, CHAIN_SPAN), 1, W // TILE + 1, jnp.int32)
    position = lax.broadcasted_iota(jnp.int32, (SUBTREE_GROUPS, CHAIN_SPAN), 1) % CHAIN
    return (jnp.where(position == CHAIN - 1, W // TILE, tile_count) * TILE).astype(jnp.int32)


def level_of(key, dims, cuts, smallest, largest):
    def one(axis_at, blocks):
        steps = jax.random.uniform(jax.random.fold_in(jax.random.fold_in(key, 6), axis_at), (blocks,), jnp.float32, smallest / len(cuts), largest / len(cuts))
        return jnp.repeat(jnp.exp(steps), dims[axis_at] // blocks).reshape((-1,) + (1,) * (len(dims) - axis_at - 1))

    gain = one(*cuts[0])
    for cut in cuts[1:]:
        gain = gain * one(*cut)
    return gain


def scatter_about(stream_key, shape, scale, reach, cuts=(), kind=jnp.bfloat16):
    values = jax.random.normal(stream_key, shape, jnp.float32) * scale
    if len(cuts) > 0:
        values = level_of(stream_key, shape, cuts, -0.22, 0.18) * values
    return jnp.clip(values, min=-reach, max=reach).astype(kind)


def setup_inputs(seed: int = 0) -> dict:
    splits = jax.random.split(jax.random.key(seed), 9)
    return {
        "right_sides": scatter_about(splits[0], (SUBTREE_GROUPS, CHAIN_SPAN, NRHS, W), 1.0, 6.0, ((0, 16), (1, 32)), jnp.float32),
        "diag_inverse": draw_diag_inverse(jax.random.fold_in(splits[8], 71), 0),
        "chain_block": draw_chain_block(jax.random.fold_in(splits[8], 71), 0),
        "top_block": scatter_about(splits[3], (SUBTREE_GROUPS, CHAIN_SPAN, P_SIZE, W), (W * DEVICES * P_SIZE // WT) ** -0.5, 0.0234375, ((0, 16), (1, 32)), jnp.float32),
        "top_rows": draw_top_rows(jax.random.fold_in(splits[8], 71), 0),
        "live_cols": draw_live_cols(jax.random.fold_in(splits[8], 71), 0),
        "top_right": scatter_about(splits[6], (NRHS, WT), 1.0, 6.0, (), jnp.float32),
        "top_inverse": draw_top_inverse(jax.random.fold_in(splits[8], 71), 0),
    }


PRECISE = lax.Precision.HIGHEST


def reference(right_sides, diag_inverse, chain_block, top_block, top_rows, live_cols, top_right, top_inverse):
    lane_count = SUBTREE_GROUPS * BRANCHES

    def to_chains(array):
        return array.reshape((lane_count, CHAIN) + array.shape[2:])

    right_all = to_chains(right_sides)
    inverse_all = to_chains(diag_inverse)
    coupling_all = to_chains(chain_block)
    across_all = to_chains(top_block)
    rows_all = to_chains(top_rows)
    live_all = to_chains(live_cols)
    columns = jnp.arange(W, dtype=jnp.int32)
    keep_all = (columns[None, None, :] < live_all[:, :, None]).astype(jnp.float32)

    def forward(carry, index):
        prior_rows, partial_value = carry
        has_child = (index > 0).astype(jnp.float32)
        pushed = jnp.einsum('lij,lrj->lri', coupling_all[:, index], prior_rows, precision=PRECISE)
        value_rows = right_all[:, index] - has_child * pushed
        forward_value = keep_all[:, index][:, None, :] * jnp.einsum('lij,lrj->lri', inverse_all[:, index], value_rows, precision=PRECISE)
        contribution = jnp.einsum('lpw,lrw->lpr', across_all[:, index], forward_value, precision=PRECISE)
        partial_value = partial_value.at[rows_all[:, index].reshape(-1)].add(contribution.reshape(-1, NRHS))
        return (forward_value, partial_value), forward_value

    start_rows = jnp.zeros((lane_count, NRHS, W), jnp.float32)
    start_partial = jnp.zeros((WT, NRHS), jnp.float32)
    (last_rows, partial_value), forward_all = lax.scan(forward, (start_rows, start_partial), jnp.arange(CHAIN, dtype=jnp.int32))

    top_mid = jnp.dot(top_right - partial_value.T, top_inverse.T, precision=PRECISE, preferred_element_type=jnp.float32)
    top_solution = jnp.dot(top_mid, top_inverse, precision=PRECISE, preferred_element_type=jnp.float32)

    def backward(above_term, index):
        has_child = (index > 0).astype(jnp.float32)
        lifted = top_solution[:, rows_all[:, index]]
        reduced = forward_all[index] - jnp.einsum('rlp,lpw->lrw', lifted, across_all[:, index], precision=PRECISE)
        masked = keep_all[:, index][:, None, :] * (reduced - above_term)
        solved = jnp.einsum('lri,lij->lrj', masked, inverse_all[:, index], precision=PRECISE)
        sent_term = has_child * jnp.einsum('lri,lij->lrj', solved, coupling_all[:, index], precision=PRECISE)
        return sent_term, solved

    _, backward_all = lax.scan(backward, jnp.zeros((lane_count, NRHS, W), jnp.float32), jnp.arange(CHAIN, dtype=jnp.int32), reverse=True)
    solution = jnp.moveaxis(backward_all, 0, 1).reshape(SUBTREE_GROUPS, CHAIN_SPAN, NRHS, W)
    return (solution, top_solution)
```

```python
import jax
import jax.numpy as jnp
from jax import lax
from jax.experimental import pallas as pl
from jax.experimental.pallas import tpu as pltpu
from jax.sharding import PartitionSpec as P

BRANCHES = 2
ROW = 4
NN = (((1,), (0,)), ((), ()))
NT = (((1,), (1,)), ((), ()))
VMEM = pl.BlockSpec(memory_space=pltpu.VMEM)
SMEM = pl.BlockSpec(memory_space=pltpu.SMEM)
F32 = jnp.float32
BF16 = jnp.bfloat16


def split(value):
    high = value.astype(BF16)
    return high, (value - high.astype(F32)).astype(BF16)


def bdot(left, right, dims):
    return lax.dot_general(left, right, dims, preferred_element_type=F32)


def dot3(left, right, dims):
    rows = left[0].shape[0]
    both = bdot(jnp.concatenate(left, 0), right[0], dims)
    return both[:rows] + both[rows:] + bdot(left[0], right[1], dims)


def kernel_call(body, outs, ins, scratch=(), flops=0, nbytes=0, limit=40):
    return pl.pallas_call(
        body,
        out_shape=outs,
        in_specs=ins,
        out_specs=jax.tree.map(lambda _: VMEM, outs),
        scratch_shapes=list(scratch),
        compiler_params=pltpu.CompilerParams(vmem_limit_bytes=limit * 2**20),
        cost_estimate=pl.CostEstimate(flops=flops, bytes_accessed=nbytes, transcendentals=0),
    )


def shape(*dims, kind=F32):
    return jax.ShapeDtypeStruct(dims, kind)


def prepare(live, right, inverse, coupling, upper, lower):
    width = inverse.shape[0]
    half = width // 2
    rhs = right.shape[0]
    count = live[0, 0]
    dh, dl = split(inverse[...])
    ch, cl = split(coupling[...])
    row = lax.broadcasted_iota(jnp.int32, (half, width), 0)
    top = dot3((dh[:half, :half], dl[:half, :half]), (ch[:half], cl[:half]), NN)
    upper[:half] = jnp.where(row < count, -top, 0.0)
    bottom = dot3((dh[half:], dl[half:]), (ch, cl), NN)
    lower[:half] = jnp.where(row + half < count, -bottom, 0.0)
    own = dot3(split(right[...]), (dh, dl), NT)
    col = lax.broadcasted_iota(jnp.int32, (rhs, width), 1)
    own = jnp.where(col < count, own, 0.0)
    upper[half:] = own[: rhs // 2]
    lower[half:] = own[rhs // 2 :]


def assemble(place, a0, b0, a1, b1, a2, b2, a3, b3, nh, nl, group, last):
    half = nh.shape[1] // 2
    rhs = group.shape[1]
    here = place[0]
    for offset, (a, b) in enumerate(((a0, b0), (a1, b1), (a2, b2), (a3, b3))):
        slot = lax.rem(here + offset, ROW)
        high, low = split(a[:half])
        nh[slot, :half] = high
        nl[slot, :half] = low
        high, low = split(b[:half])
        nh[slot, half:] = high
        nl[slot, half:] = low
        group[slot, : rhs // 2] = a[half:]
        group[slot, rhs // 2 :] = b[half:]
    value = group[0]
    for j in range(1, ROW):
        value = group[j] + dot3(split(value), (nh[j], nl[j]), NT)
        group[j] = value
    last[...] = value


def multiply_up(place, nh, nl, qh, ql, ph, plow):
    here = place[0]
    high, low = nh[0], nl[0]

    @pl.when(here == 0)
    def _():
        qh[...] = high
        ql[...] = low

    for j in range(1, ROW):
        high, low = split(dot3((nh[j], nl[j]), (high, low), NN))

        @pl.when(here == j)
        def _():
            qh[...] = high
            ql[...] = low

    ph[...] = high
    plow[...] = low


def hop_forward(base, coming, ph, plow, out):
    out[...] = base[...] + dot3(split(coming[...]), (ph[...], plow[...]), NT)


def hop_backward(base, coming, ph, plow, out):
    out[...] = base[...] + dot3(split(coming[...]), (ph[...], plow[...]), NN)


def onehot_of(rows, top):
    return (lax.broadcasted_iota(jnp.int32, (top, rows.shape[1]), 0) == rows[...]).astype(F32).astype(BF16)


def contribute(place, group, coming, qh, ql, across, rows, solved, tiles):
    here = place[0]
    value = group[here] + dot3(split(coming[...]), (qh[...], ql[...]), NT)
    solved[...] = value
    pushed = dot3(split(value), split(across[...]), NT)
    count, top_rows_, lanes = tiles.shape
    col_blocks = count // (value.shape[0] // top_rows_)
    onehot = onehot_of(rows, col_blocks * lanes)
    high, low = split(pushed)
    both = bdot(jnp.concatenate((high, low), 0), onehot, NT)
    total = both[: value.shape[0]] + both[value.shape[0] :]
    for piece in range(count):
        r, c = piece // col_blocks, piece % col_blocks
        tiles[piece] = total[r * top_rows_ : (r + 1) * top_rows_, c * lanes : (c + 1) * lanes]


def total_of(tiles, out):
    value = tiles[0]
    for piece in range(1, tiles.shape[0]):
        value = value + tiles[piece]
    for piece in range(out.shape[0]):
        out[piece] = value


def solve_top(tiles, top_right, weights, rows, solved, across, top_out, reduced):
    count, tile_rows, lanes = tiles.shape
    rhs, top = top_right.shape
    col_blocks = top // lanes
    lines = []
    for r in range(rhs // tile_rows):
        lines.append(jnp.concatenate([tiles[r * col_blocks + c] for c in range(col_blocks)], 1))
    rest = top_right[...] - jnp.concatenate(lines, 0)
    blocks, _, block_cols = weights.shape
    pairs = [split(weights[j]) for j in range(blocks)]
    mid = jnp.zeros((rhs, top), F32)
    for j in range(blocks):
        mid = mid + dot3(split(rest[:, j * block_cols : (j + 1) * block_cols]), pairs[j], NT)
    mid = split(mid)
    answer = jnp.concatenate([dot3(mid, pairs[j], NN) for j in range(blocks)], 1)
    top_out[...] = answer
    onehot = onehot_of(rows, top)
    high, low = split(answer)
    both = bdot(jnp.concatenate((high, low), 0), onehot, NN)
    lifted = both[:rhs] + both[rhs:]
    value = solved[...] - dot3(split(lifted), split(across[...]), NN)
    for piece in range(reduced.shape[0]):
        reduced[piece] = value


def row_backward(place, reduced, nh, nl, own, sent):
    here = place[0]
    value = reduced[ROW - 1]
    for j in range(ROW - 1, -1, -1):
        if j < ROW - 1:
            value = reduced[j] + value

        @pl.when(here == j)
        def _():
            own[...] = value

        value = dot3(split(value), (nh[j], nl[j]), NN)
    sent[...] = value


def finish(place, live, own, coming, nh, nl, inverse, out, term):
    here = place[0]
    term[...] = coming[...]
    for j in range(ROW - 1, 0, -1):

        @pl.when(here < j)
        def _():
            term[...] = dot3(split(term[...]), (nh[j], nl[j]), NN)

    value = own[...] + term[...]
    col = lax.broadcasted_iota(jnp.int32, value.shape, 1)
    value = jnp.where(col < live[0, 0], value, 0.0)
    out[...] = dot3(split(value), split(inverse[...]), NN)


def shards(
    right_sides, diag_inverse, chain_block, top_block, top_rows, live_cols, top_right, top_inverse
):
    ga, gz = lax.axis_size("ga"), lax.axis_size("gz")
    chain_len = ga // BRANCHES
    chain_rows = chain_len // ROW
    index = lax.axis_index("ga")
    place = (index % ROW).astype(jnp.int32)[None]
    right, inverse = right_sides[0, 0], diag_inverse[0, 0]
    coupling, across = chain_block[0, 0], top_block[0, 0]
    rows = top_rows[0]
    rhs, width = right.shape
    top = top_right.shape[1]
    x_groups = [[r * ROW + c for c in range(ROW)] for r in range(ga // ROW)]
    y_groups = [[r * ROW + c for r in range(ga // ROW)] for c in range(ROW)]

    def ring(value, step):
        return lax.ppermute(
            value, "ga", [(i, i // ROW * ROW + (i + step) % ROW) for i in range(ga)]
        )

    def hop(value, step):
        route = [
            (i, i + step * ROW)
            for i in range(ga)
            if 0 <= i // ROW % chain_rows + step < chain_rows
        ]
        return lax.ppermute(value, "ga", route)

    def pair(*dims):
        return (shape(*dims, kind=BF16), shape(*dims, kind=BF16))

    level = lax.axis_index("gz")
    tile = 8
    wide = top // (gz // (top_inverse.shape[0] // tile))
    ways = top_inverse.shape[0] // tile
    piece = lax.dynamic_slice(
        top_inverse, (level % ways * tile, level // ways * wide), (tile, wide)
    )
    piece = lax.all_gather(piece, "ga", axis_index_groups=y_groups)
    piece = lax.all_gather(piece, "ga", axis_index_groups=x_groups)
    weights = lax.all_gather(piece, "gz").reshape(gz // ways, top, wide)

    half = width // 2 + rhs // 2
    a0, b0 = kernel_call(
        prepare,
        (shape(half, width), shape(half, width)),
        [SMEM, VMEM, VMEM, VMEM],
        flops=6 * width**3,
        nbytes=16 * width**2,
    )(live_cols, right, inverse, coupling)
    a3 = ring(a0, 1)
    b1 = ring(b0, -1)
    b3 = ring(b0, 1)
    a1 = ring(a0, -1)
    a2 = ring(a3, 1)
    b2 = ring(b1, -1)

    nh, nl, group, last = kernel_call(
        assemble,
        pair(ROW, width, width) + (shape(ROW, rhs, width), shape(rhs, width)),
        [SMEM] + [VMEM] * 8,
        flops=24 * rhs * width**2,
        nbytes=32 * width**2,
    )(place, a0, b0, a1, b1, a2, b2, a3, b3)
    coming = hop(last, 1)
    qh, ql, ph, plow = kernel_call(
        multiply_up,
        pair(width, width) * 2,
        [SMEM, VMEM, VMEM],
        flops=18 * width**3,
        nbytes=24 * width**2,
    )(place, nh, nl)
    for _ in range(chain_rows - 2):
        moved = kernel_call(
            hop_forward, shape(rhs, width), [VMEM] * 4, flops=6 * rhs * width**2
        )(last, coming, ph, plow)
        coming = hop(moved, 1)

    pieces = ga
    tiles = (pieces, rhs * top // pieces // 128, 128)
    solved, partial = kernel_call(
        contribute,
        (shape(rhs, width), shape(*tiles)),
        [SMEM] + [VMEM] * 6,
        flops=12 * rhs * width**2,
    )(place, group, coming, qh, ql, across, rows)
    partial = lax.all_to_all(partial, "ga", 0, 0)
    partial = kernel_call(total_of, shape(gz, *tiles[1:]), [VMEM])(partial)
    partial = lax.all_to_all(partial, "gz", 0, 0)
    partial = kernel_call(total_of, shape(*tiles), [VMEM])(partial)
    partial = lax.all_to_all(partial, "ga", 0, 0)
    top_solution, reduced = kernel_call(
        solve_top,
        (shape(rhs, top), shape(ROW, rhs, width)),
        [VMEM] * 6,
        flops=12 * rhs * top**2,
    )(partial, top_right, weights, rows, solved, across)

    reduced = lax.all_to_all(reduced, "ga", 0, 0, axis_index_groups=x_groups)
    own, sent = kernel_call(
        row_backward,
        (shape(rhs, width), shape(rhs, width)),
        [SMEM] + [VMEM] * 3,
        flops=24 * rhs * width**2,
    )(place, reduced, nh, nl)
    coming = hop(sent, -1)
    for _ in range(chain_rows - 2):
        moved = kernel_call(
            hop_backward, shape(rhs, width), [VMEM] * 4, flops=6 * rhs * width**2
        )(sent, coming, ph, plow)
        coming = hop(moved, -1)
    result = kernel_call(
        finish,
        shape(rhs, width),
        [SMEM, SMEM] + [VMEM] * 5,
        scratch=[pltpu.VMEM((rhs, width), F32)],
        flops=24 * rhs * width**2,
    )(place, live_cols, own, coming, nh, nl, inverse)
    return (result[None, None], top_solution)


def solution(mesh):
    placed = (
        P("gz", "ga", None, None),
        P("gz", "ga", None, None),
        P("gz", "ga", None, None),
        P("gz", "ga", None, None),
        P("gz", "ga", None),
        P("gz", "ga"),
        P(),
        P("ga", None),
    )
    return jax.shard_map(
        shards,
        mesh=mesh,
        in_specs=placed,
        out_specs=(P("gz", "ga", None, None), P()),
        check_vma=False,
    )
```

```python
import jax
import jax.numpy as jnp
from jax import lax
from jax.experimental import pallas as pl
from jax.experimental.pallas import tpu as pltpu
from jax.sharding import PartitionSpec as P

BRANCHES = 2
ROW = 4
NN = (((1,), (0,)), ((), ()))
NT = (((1,), (1,)), ((), ()))
VMEM = pl.BlockSpec(memory_space=pltpu.VMEM)
SMEM = pl.BlockSpec(memory_space=pltpu.SMEM)
HBM = pl.BlockSpec(memory_space=pltpu.HBM)
F32 = jnp.float32
BF16 = jnp.bfloat16


def split(value):
    high = value.astype(BF16)
    return high, (value - high.astype(F32)).astype(BF16)


def bdot(left, right, dims):
    return lax.dot_general(left, right, dims, preferred_element_type=F32)


def dot3(left, right, dims):
    rows = left[0].shape[0]
    both = bdot(jnp.concatenate(left, 0), right[0], dims)
    return both[:rows] + both[rows:] + bdot(left[0], right[1], dims)


def kernel_call(body, outs, ins, scratch=(), flops=0, nbytes=0, limit=16):
    return pl.pallas_call(
        body,
        out_shape=outs,
        in_specs=ins,
        out_specs=jax.tree.map(lambda _: VMEM, outs),
        scratch_shapes=list(scratch),
        compiler_params=pltpu.CompilerParams(vmem_limit_bytes=limit * 2**20),
        cost_estimate=pl.CostEstimate(flops=flops, bytes_accessed=nbytes, transcendentals=0),
    )


def shape(*dims, kind=F32):
    return jax.ShapeDtypeStruct(dims, kind)


def prepare(live, right_hbm, inverse_hbm, coupling_hbm, upper, lower, right, inverse, coupling, sems):
    width = inverse.shape[0]
    half = width // 2
    rhs = right.shape[0]
    halves = (pl.ds(0, half), pl.ds(half, half))
    moves = [
        pltpu.make_async_copy(inverse_hbm, inverse, sems.at[0]),
        pltpu.make_async_copy(coupling_hbm.at[halves[0]], coupling.at[halves[0]], sems.at[1]),
        pltpu.make_async_copy(coupling_hbm.at[halves[1]], coupling.at[halves[1]], sems.at[2]),
        pltpu.make_async_copy(right_hbm, right, sems.at[3]),
    ]
    for move in moves:
        move.start()
    count = live[0, 0]
    row = lax.broadcasted_iota(jnp.int32, (half, width), 0)
    moves[0].wait()
    dh, dl = split(inverse[...])
    moves[1].wait()
    ch, cl = split(coupling[:half])
    top = dot3((dh[:half, :half], dl[:half, :half]), (ch, cl), NN)
    upper[:half] = jnp.where(row < count, -top, 0.0)
    bottom = dot3((dh[half:, :half], dl[half:, :half]), (ch, cl), NN)
    moves[2].wait()
    ch, cl = split(coupling[half:])
    bottom = bottom + dot3((dh[half:, half:], dl[half:, half:]), (ch, cl), NN)
    lower[:half] = jnp.where(row + half < count, -bottom, 0.0)
    moves[3].wait()
    own = dot3(split(right[...]), (dh, dl), NT)
    col = lax.broadcasted_iota(jnp.int32, (rhs, width), 1)
    own = jnp.where(col < count, own, 0.0)
    upper[half:] = own[: rhs // 2]
    lower[half:] = own[rhs // 2 :]


def pack_lower(blocks, out):
    start = 0
    for y in range(blocks.shape[0]):
        wide = (y + 1) * blocks.shape[2] // blocks.shape[0]
        out[:, start : start + wide] = blocks[y, :, :wide]
        start += wide


def place_block(a, b, slot, nh, nl, group):
    half = nh.shape[1] // 2
    rhs = group.shape[1]
    high, low = split(a[:half])
    nh[slot, :half] = high
    nl[slot, :half] = low
    high, low = split(b[:half])
    nh[slot, half:] = high
    nl[slot, half:] = low
    group[slot, : rhs // 2] = a[half:]
    group[slot, rhs // 2 :] = b[half:]


def stage(a0, b0, a1, b1, a3, b3, nh, nl, group):
    for slot, (a, b) in enumerate(((a0, b0), (a1, b1), (a3, b3))):
        place_block(a, b, slot, nh, nl, group)


def assemble(place, sh, sl, sgroup, a2, b2, nh, nl, group, last):
    here = place[0]
    for at, offset in enumerate((0, 1, 3)):
        slot = lax.rem(here + offset, ROW)
        nh[slot] = sh[at]
        nl[slot] = sl[at]
        group[slot] = sgroup[at]
    place_block(a2, b2, lax.rem(here + 2, ROW), nh, nl, group)
    value = group[0]
    for j in range(1, ROW):
        value = group[j] + dot3(split(value), (nh[j], nl[j]), NT)
        group[j] = value
    last[...] = value


def multiply_up(place, nh, nl, qh, ql, ph, plow):
    here = place[0]
    high, low = nh[0], nl[0]

    @pl.when(here == 0)
    def _():
        qh[...] = high
        ql[...] = low

    for j in range(1, ROW):
        high, low = split(dot3((nh[j], nl[j]), (high, low), NN))

        @pl.when(here == j)
        def _():
            qh[...] = high
            ql[...] = low

    ph[...] = high
    plow[...] = low


def hop_forward(base, coming, ph, plow, out):
    out[...] = base[...] + dot3(split(coming[...]), (ph[...], plow[...]), NT)


def hop_backward(base, coming, ph, plow, out):
    out[...] = base[...] + dot3(split(coming[...]), (ph[...], plow[...]), NN)


def onehot_of(rows, top):
    return (lax.broadcasted_iota(jnp.int32, (top, rows.shape[1]), 0) == rows[...]).astype(F32).astype(BF16)


def contribute(place, group, coming, qh, ql, across, rows, solved, tiles):
    here = place[0]
    value = group[here] + dot3(split(coming[...]), (qh[...], ql[...]), NT)
    solved[...] = value
    pushed = dot3(split(value), split(across[...]), NT)
    count, depth, lanes = tiles.shape
    col_blocks = count * depth // value.shape[0]
    high, low = split(pushed)
    both = bdot(jnp.concatenate((high, low), 0), onehot_of(rows, col_blocks * lanes), NT)
    total = both[: value.shape[0]] + both[value.shape[0] :]
    for tile in range(count):
        r, c = tile // col_blocks, tile % col_blocks
        tiles[tile] = total[r * depth : (r + 1) * depth, c * lanes : (c + 1) * lanes]


def total_of(pieces, out):
    value = pieces[0]
    for piece in range(1, pieces.shape[0]):
        value = value + pieces[piece]
    for piece in range(out.shape[0]):
        out[piece] = value


def solve_top(
    tiles, top_right, packed_hbm, across_hbm, rows, solved, top_out, reduced, packed, across, wh, wl, sems
):
    count, depth, lanes = tiles.shape
    rhs, top = top_right.shape
    col_blocks = top // lanes
    steps = packed.shape[1] * packed.shape[0]
    moves = []
    start = 0
    for step in range(top // steps):
        wide = (step + 1) * steps
        part = (slice(None), slice(None), pl.ds(start, wide))
        moves.append(
            pltpu.make_async_copy(packed_hbm.at[part], packed.at[part], sems.at[step])
        )
        start += wide
    moves.append(pltpu.make_async_copy(across_hbm, across, sems.at[top // steps]))
    for move in moves:
        move.start()
    lines = []
    for r in range(rhs // depth):
        lines.append(jnp.concatenate([tiles[r * col_blocks + c] for c in range(col_blocks)], 1))
    rest = split(top_right[...] - jnp.concatenate(lines, 0))
    block = 2 * steps
    mid = []
    start = 0
    for step in range(top // steps):
        wide = (step + 1) * steps
        moves[step].wait()
        high, low = split(packed[:, :, start : start + wide].reshape(steps, wide))
        at = slice(step * steps, (step + 1) * steps)
        wh[at, :wide] = high
        wl[at, :wide] = low
        start += wide
        if step % 2 == 0:
            wh[at, wide : wide + steps] = jnp.zeros((steps, steps), BF16)
            wl[at, wide : wide + steps] = jnp.zeros((steps, steps), BF16)
        else:
            at = slice(wide - block, wide)
            mid.append(
                dot3((rest[0][:, :wide], rest[1][:, :wide]), (wh[at, :wide], wl[at, :wide]), NT)
            )
    mid = split(jnp.concatenate(mid, 1))
    answer = []
    for j in range(0, top, block):
        end = j + block
        answer.append(
            dot3((mid[0][:, j:], mid[1][:, j:]), (wh[j:, j:end], wl[j:, j:end]), NN)
        )
    answer = jnp.concatenate(answer, 1)
    top_out[...] = answer
    high, low = split(answer)
    both = bdot(jnp.concatenate((high, low), 0), onehot_of(rows, top), NN)
    lifted = both[:rhs] + both[rhs:]
    moves[-1].wait()
    value = solved[...] - dot3(split(lifted), split(across[...]), NN)
    for piece in range(reduced.shape[0]):
        reduced[piece] = value


def row_backward(place, reduced, nh, nl, own, sent):
    here = place[0]
    value = reduced[ROW - 1]
    for j in range(ROW - 1, -1, -1):
        if j < ROW - 1:
            value = reduced[j] + value

        @pl.when(here == j)
        def _():
            own[...] = value

        value = dot3(split(value), (nh[j], nl[j]), NN)
    sent[...] = value


def finish(place, live, own, coming, nh, nl, inverse, out, term):
    here = place[0]
    term[...] = coming[...]
    for j in range(ROW - 1, 0, -1):

        @pl.when(here < j)
        def _():
            term[...] = dot3(split(term[...]), (nh[j], nl[j]), NN)

    value = own[...] + term[...]
    col = lax.broadcasted_iota(jnp.int32, value.shape, 1)
    value = jnp.where(col < live[0, 0], value, 0.0)
    out[...] = dot3(split(value), split(inverse[...]), NN)


def shards(
    right_sides, diag_inverse, chain_block, top_block, top_rows, live_cols, top_right, top_inverse
):
    ga, gz = lax.axis_size("ga"), lax.axis_size("gz")
    chain_len = ga // BRANCHES
    chain_rows = chain_len // ROW
    index = lax.axis_index("ga")
    place = (index % ROW).astype(jnp.int32)[None]
    right, inverse = right_sides[0, 0], diag_inverse[0, 0]
    coupling, across = chain_block[0, 0], top_block[0, 0]
    rows = top_rows[0]
    rhs, width = right.shape
    top = top_right.shape[1]
    x_groups = [[r * ROW + c for c in range(ROW)] for r in range(ga // ROW)]
    y_groups = [[r * ROW + c for r in range(ga // ROW)] for c in range(ROW)]

    def ring(value, step):
        return lax.ppermute(
            value, "ga", [(i, i // ROW * ROW + (i + step) % ROW) for i in range(ga)]
        )

    def hop(value, step):
        route = [
            (i, i + step * ROW)
            for i in range(ga)
            if 0 <= i // ROW % chain_rows + step < chain_rows
        ]
        return lax.ppermute(value, "ga", route)

    def pair(*dims):
        return (shape(*dims, kind=BF16), shape(*dims, kind=BF16))

    blocks = lax.all_gather(top_inverse, "ga", axis_index_groups=y_groups)
    half = width // 2 + rhs // 2
    a0, b0 = kernel_call(
        prepare,
        (shape(half, width), shape(half, width)),
        [SMEM, HBM, HBM, HBM],
        scratch=[
            pltpu.VMEM((rhs, width), F32),
            pltpu.VMEM((width, width), F32),
            pltpu.VMEM((width, width), F32),
            pltpu.SemaphoreType.DMA((4,)),
        ],
        flops=6 * width**3,
        nbytes=16 * width**2,
        limit=60,
    )(live_cols, right, inverse, coupling)
    a3 = ring(a0, 1)
    b1 = ring(b0, -1)
    b3 = ring(b0, 1)
    a1 = ring(a0, -1)
    a2 = ring(a3, 1)
    b2 = ring(b1, -1)

    staged = kernel_call(
        stage,
        pair(ROW - 1, width, width) + (shape(ROW - 1, rhs, width),),
        [VMEM] * 6,
        nbytes=32 * width**2,
    )(a0, b0, a1, b1, a3, b3)
    nh, nl, group, last = kernel_call(
        assemble,
        pair(ROW, width, width) + (shape(ROW, rhs, width), shape(rhs, width)),
        [SMEM] + [VMEM] * 5,
        flops=24 * rhs * width**2,
        nbytes=32 * width**2,
    )(place, *staged, a2, b2)
    coming = hop(last, 1)
    qh, ql, ph, plow = kernel_call(
        multiply_up,
        pair(width, width) * 2,
        [SMEM, VMEM, VMEM],
        flops=18 * width**3,
        nbytes=24 * width**2,
    )(place, nh, nl)
    for step in range(chain_rows - 2):
        moved = kernel_call(
            hop_forward, shape(rhs, width), [VMEM] * 4, flops=6 * rhs * width**2
        )(last, coming, ph, plow)
        if step == 0:
            blocks, moved = lax.optimization_barrier((blocks, moved))
        coming = hop(moved, 1)
    packed = kernel_call(
        pack_lower,
        shape(top_inverse.shape[0], top * (ga // ROW + 1) // 2),
        [VMEM],
        nbytes=2 * top**2,
    )(blocks)
    packed = lax.all_gather(packed, "ga", axis_index_groups=x_groups)

    tiles = (ga, rhs * top // ga // 128, 128)
    solved, partial = kernel_call(
        contribute,
        (shape(rhs, width), shape(*tiles)),
        [SMEM] + [VMEM] * 6,
        flops=12 * rhs * width**2,
    )(place, group, coming, qh, ql, across, rows)
    partial = lax.all_to_all(partial, "ga", 0, 0)
    partial = kernel_call(total_of, shape(gz, *tiles[1:]), [VMEM])(partial)
    partial = lax.all_to_all(partial, "gz", 0, 0)
    partial = kernel_call(total_of, shape(*tiles), [VMEM])(partial)
    partial = lax.all_to_all(partial, "ga", 0, 0)
    partial, packed = lax.optimization_barrier((partial, packed))
    top_solution, reduced = kernel_call(
        solve_top,
        (shape(rhs, top), shape(ROW, rhs, width)),
        [VMEM, VMEM, HBM, HBM, VMEM, VMEM],
        scratch=[
            pltpu.VMEM(packed.shape, F32),
            pltpu.VMEM(across.shape, F32),
            pltpu.VMEM((top, top), BF16),
            pltpu.VMEM((top, top), BF16),
            pltpu.SemaphoreType.DMA((ga // ROW + 1,)),
        ],
        flops=12 * rhs * top**2,
        limit=24,
    )(partial, top_right, packed, across, rows, solved)

    reduced = lax.all_to_all(reduced, "ga", 0, 0, axis_index_groups=x_groups)
    own, sent = kernel_call(
        row_backward,
        (shape(rhs, width), shape(rhs, width)),
        [SMEM] + [VMEM] * 3,
        flops=24 * rhs * width**2,
    )(place, reduced, nh, nl)
    coming = hop(sent, -1)
    for _ in range(chain_rows - 2):
        moved = kernel_call(
            hop_backward, shape(rhs, width), [VMEM] * 4, flops=6 * rhs * width**2
        )(sent, coming, ph, plow)
        coming = hop(moved, -1)
    result = kernel_call(
        finish,
        shape(rhs, width),
        [SMEM, SMEM] + [VMEM] * 5,
        scratch=[pltpu.VMEM((rhs, width), F32)],
        flops=24 * rhs * width**2,
    )(place, live_cols, own, coming, nh, nl, inverse)
    return (result[None, None], top_solution)


def solution(mesh):
    placed = (
        P("gz", "ga", None, None),
        P("gz", "ga", None, None),
        P("gz", "ga", None, None),
        P("gz", "ga", None, None),
        P("gz", "ga", None),
        P("gz", "ga"),
        P(),
        P("ga", None),
    )
    return jax.shard_map(
        shards,
        mesh=mesh,
        in_specs=placed,
        out_specs=(P("gz", "ga", None, None), P()),
        check_vma=False,
    )
```

```python
import jax
import jax.numpy as jnp
from jax import lax
from jax.experimental import pallas as pl
from jax.experimental.pallas import tpu as pltpu
from jax.sharding import PartitionSpec as P

BRANCHES = 2
ROW = 4
NN = (((1,), (0,)), ((), ()))
NT = (((1,), (1,)), ((), ()))
VMEM = pl.BlockSpec(memory_space=pltpu.VMEM)
SMEM = pl.BlockSpec(memory_space=pltpu.SMEM)
HBM = pl.BlockSpec(memory_space=pltpu.HBM)
F32 = jnp.float32
BF16 = jnp.bfloat16


def split(value):
    high = value.astype(BF16)
    return high, (value - high.astype(F32)).astype(BF16)


def bdot(left, right, dims):
    return lax.dot_general(left, right, dims, preferred_element_type=F32)


def dot3(left, right, dims):
    rows = left[0].shape[0]
    both = bdot(jnp.concatenate(left, 0), right[0], dims)
    return both[:rows] + both[rows:] + bdot(left[0], right[1], dims)


def place_in_row():
    return lax.rem(lax.axis_index("ga"), ROW)


def kernel_call(body, outs, ins, scratch=(), flops=0, nbytes=0, limit=16):
    return pl.pallas_call(
        body,
        out_shape=outs,
        in_specs=ins,
        out_specs=jax.tree.map(lambda _: VMEM, outs),
        scratch_shapes=list(scratch),
        compiler_params=pltpu.CompilerParams(vmem_limit_bytes=limit * 2**20),
        cost_estimate=pl.CostEstimate(flops=flops, bytes_accessed=nbytes, transcendentals=0),
    )


def shape(*dims, kind=F32):
    return jax.ShapeDtypeStruct(dims, kind)


def prepare(live, right_hbm, inverse_hbm, coupling_hbm, upper, lower, right, inverse, coupling, sems):
    width = inverse.shape[0]
    half = width // 2
    rhs = right.shape[0]
    halves = (pl.ds(0, half), pl.ds(half, half))
    moves = [
        pltpu.make_async_copy(inverse_hbm, inverse, sems.at[0]),
        pltpu.make_async_copy(coupling_hbm.at[halves[0]], coupling.at[halves[0]], sems.at[1]),
        pltpu.make_async_copy(coupling_hbm.at[halves[1]], coupling.at[halves[1]], sems.at[2]),
        pltpu.make_async_copy(right_hbm, right, sems.at[3]),
    ]
    for move in moves:
        move.start()
    count = live[0, 0]
    row = lax.broadcasted_iota(jnp.int32, (half, width), 0)
    moves[0].wait()
    dh, dl = split(inverse[...])
    moves[1].wait()
    ch, cl = split(coupling[:half])
    top = dot3((dh[:half, :half], dl[:half, :half]), (ch, cl), NN)
    upper[:half] = jnp.where(row < count, -top, 0.0)
    bottom = dot3((dh[half:, :half], dl[half:, :half]), (ch, cl), NN)
    moves[2].wait()
    ch, cl = split(coupling[half:])
    bottom = bottom + dot3((dh[half:, half:], dl[half:, half:]), (ch, cl), NN)
    lower[:half] = jnp.where(row + half < count, -bottom, 0.0)
    moves[3].wait()
    own = dot3(split(right[...]), (dh, dl), NT)
    col = lax.broadcasted_iota(jnp.int32, (rhs, width), 1)
    own = jnp.where(col < count, own, 0.0)
    upper[half:] = own[: rhs // 2]
    lower[half:] = own[rhs // 2 :]


def pack_lower(blocks, out):
    start = 0
    for y in range(blocks.shape[0]):
        wide = (y + 1) * blocks.shape[2] // blocks.shape[0]
        out[:, start : start + wide] = blocks[y, :, :wide]
        start += wide


def place_block(a, b, slot, nh, nl, group):
    half = nh.shape[1] // 2
    rhs = group.shape[1]
    high, low = split(a[:half])
    nh[slot, :half] = high
    nl[slot, :half] = low
    high, low = split(b[:half])
    nh[slot, half:] = high
    nl[slot, half:] = low
    group[slot, : rhs // 2] = a[half:]
    group[slot, rhs // 2 :] = b[half:]


def stage(a0, b0, a1, b1, a3, b3, nh, nl, group):
    for slot, (a, b) in enumerate(((a0, b0), (a1, b1), (a3, b3))):
        place_block(a, b, slot, nh, nl, group)


def assemble(sh, sl, sgroup, a2, b2, nh, nl, group, last):
    here = place_in_row()
    for at, offset in enumerate((0, 1, 3)):
        slot = lax.rem(here + offset, ROW)
        nh[slot] = sh[at]
        nl[slot] = sl[at]
        group[slot] = sgroup[at]
    place_block(a2, b2, lax.rem(here + 2, ROW), nh, nl, group)
    value = group[0]
    for j in range(1, ROW):
        value = group[j] + dot3(split(value), (nh[j], nl[j]), NT)
        group[j] = value
    last[...] = value


def multiply_up(nh, nl, qh, ql, ph, plow):
    here = place_in_row()
    high, low = nh[0], nl[0]

    @pl.when(here == 0)
    def _():
        qh[...] = high
        ql[...] = low

    for j in range(1, ROW):
        high, low = split(dot3((nh[j], nl[j]), (high, low), NN))

        @pl.when(here == j)
        def _():
            qh[...] = high
            ql[...] = low

    ph[...] = high
    plow[...] = low


def hop_forward(base, coming, ph, plow, out):
    out[...] = base[...] + dot3(split(coming[...]), (ph[...], plow[...]), NT)


def hop_backward(base, coming, ph, plow, out):
    out[...] = base[...] + dot3(split(coming[...]), (ph[...], plow[...]), NN)


def onehot_of(rows, top):
    return (lax.broadcasted_iota(jnp.int32, (top, rows.shape[1]), 0) == rows[...]).astype(F32).astype(BF16)


def contribute(group, coming, qh, ql, across, rows, top_right, solved, tiles):
    here = place_in_row()
    value = group[here] + dot3(split(coming[...]), (qh[...], ql[...]), NT)
    solved[...] = value
    pushed = dot3(split(value), split(across[...]), NT)
    count, depth, lanes = tiles.shape
    col_blocks = count * depth // value.shape[0]
    high, low = split(pushed)
    both = bdot(jnp.concatenate((high, low), 0), onehot_of(rows, col_blocks * lanes), NT)
    total = both[: value.shape[0]] + both[value.shape[0] :]
    first = (lax.axis_index("gz") == 0) & (lax.axis_index("ga") == 0)
    total = jnp.where(first, top_right[...] - total, -total)
    for tile in range(count):
        r, c = tile // col_blocks, tile % col_blocks
        tiles[tile] = total[r * depth : (r + 1) * depth, c * lanes : (c + 1) * lanes]


def total_of(pieces, out):
    value = pieces[0]
    for piece in range(1, pieces.shape[0]):
        value = value + pieces[piece]
    for piece in range(out.shape[0]):
        out[piece] = value


def solve_top(tiles, packed, top_out, wh, wl):
    count, depth, lanes = tiles.shape
    rhs, top = top_out.shape
    col_blocks = top // lanes
    steps = packed.shape[1] * packed.shape[0]
    lines = []
    for r in range(rhs // depth):
        lines.append(jnp.concatenate([tiles[r * col_blocks + c] for c in range(col_blocks)], 1))
    rest = split(jnp.concatenate(lines, 0))
    block = 2 * steps
    mid = []
    start = 0
    for step in range(top // steps):
        wide = (step + 1) * steps
        high, low = split(packed[:, :, start : start + wide].reshape(steps, wide))
        at = slice(step * steps, (step + 1) * steps)
        wh[at, :wide] = high
        wl[at, :wide] = low
        start += wide
        if step % 2 == 0:
            wh[at, wide : wide + steps] = jnp.zeros((steps, steps), BF16)
            wl[at, wide : wide + steps] = jnp.zeros((steps, steps), BF16)
        else:
            at = slice(wide - block, wide)
            mid.append(
                dot3((rest[0][:, :wide], rest[1][:, :wide]), (wh[at, :wide], wl[at, :wide]), NT)
            )
    mid = split(jnp.concatenate(mid, 1))
    answer = []
    for j in range(0, top, block):
        end = j + block
        answer.append(
            dot3((mid[0][:, j:], mid[1][:, j:]), (wh[j:, j:end], wl[j:, j:end]), NN)
        )
    top_out[...] = jnp.concatenate(answer, 1)


def lift(top_out, across, rows, solved, reduced):
    rhs, top = top_out.shape
    high, low = split(top_out[...])
    both = bdot(jnp.concatenate((high, low), 0), onehot_of(rows, top), NN)
    lifted = both[:rhs] + both[rhs:]
    value = solved[...] - dot3(split(lifted), split(across[...]), NN)
    for piece in range(reduced.shape[0]):
        reduced[piece] = value


def row_backward(reduced, nh, nl, own, sent):
    here = place_in_row()
    value = reduced[ROW - 1]
    for j in range(ROW - 1, -1, -1):
        if j < ROW - 1:
            value = reduced[j] + value

        @pl.when(here == j)
        def _():
            own[...] = value

        value = dot3(split(value), (nh[j], nl[j]), NN)
    sent[...] = value


def finish(live, own, coming, nh, nl, inverse, out, term):
    here = place_in_row()
    term[...] = coming[...]
    for j in range(ROW - 1, 0, -1):

        @pl.when(here < j)
        def _():
            term[...] = dot3(split(term[...]), (nh[j], nl[j]), NN)

    value = own[...] + term[...]
    col = lax.broadcasted_iota(jnp.int32, value.shape, 1)
    value = jnp.where(col < live[0, 0], value, 0.0)
    out[...] = dot3(split(value), split(inverse[...]), NN)


def shards(
    right_sides, diag_inverse, chain_block, top_block, top_rows, live_cols, top_right, top_inverse
):
    ga, gz = lax.axis_size("ga"), lax.axis_size("gz")
    chain_len = ga // BRANCHES
    chain_rows = chain_len // ROW
    right, inverse = right_sides[0, 0], diag_inverse[0, 0]
    coupling, across = chain_block[0, 0], top_block[0, 0]
    rows = top_rows[0]
    rhs, width = right.shape
    top = top_right.shape[1]
    x_groups = [[r * ROW + c for c in range(ROW)] for r in range(ga // ROW)]
    y_groups = [[r * ROW + c for r in range(ga // ROW)] for c in range(ROW)]

    def ring(value, step):
        return lax.ppermute(
            value, "ga", [(i, i // ROW * ROW + (i + step) % ROW) for i in range(ga)]
        )

    def hop(value, step):
        route = [
            (i, i + step * ROW)
            for i in range(ga)
            if 0 <= i // ROW % chain_rows + step < chain_rows
        ]
        return lax.ppermute(value, "ga", route)

    def pair(*dims):
        return (shape(*dims, kind=BF16), shape(*dims, kind=BF16))

    half = width // 2 + rhs // 2
    a0, b0 = kernel_call(
        prepare,
        (shape(half, width), shape(half, width)),
        [SMEM, HBM, HBM, HBM],
        scratch=[
            pltpu.VMEM((rhs, width), F32),
            pltpu.VMEM((width, width), F32),
            pltpu.VMEM((width, width), F32),
            pltpu.SemaphoreType.DMA((4,)),
        ],
        flops=6 * width**3,
        nbytes=16 * width**2,
        limit=60,
    )(live_cols, right, inverse, coupling)
    top_inverse, a0 = lax.optimization_barrier((top_inverse, a0))
    blocks = lax.all_gather(top_inverse, "ga", axis_index_groups=y_groups)
    a3 = ring(a0, 1)
    b1 = ring(b0, -1)
    b3 = ring(b0, 1)
    a1 = ring(a0, -1)
    a2 = ring(a3, 1)
    b2 = ring(b1, -1)

    staged = kernel_call(
        stage,
        pair(ROW - 1, width, width) + (shape(ROW - 1, rhs, width),),
        [VMEM] * 6,
        nbytes=32 * width**2,
    )(a0, b0, a1, b1, a3, b3)
    nh, nl, group, last = kernel_call(
        assemble,
        pair(ROW, width, width) + (shape(ROW, rhs, width), shape(rhs, width)),
        [VMEM] * 5,
        flops=24 * rhs * width**2,
        nbytes=32 * width**2,
    )(*staged, a2, b2)
    coming = hop(last, 1)
    qh, ql, ph, plow = kernel_call(
        multiply_up,
        pair(width, width) * 2,
        [VMEM, VMEM],
        flops=18 * width**3,
        nbytes=24 * width**2,
    )(nh, nl)
    blocks, coming, plow = lax.optimization_barrier((blocks, coming, plow))
    packed = kernel_call(
        pack_lower,
        shape(top_inverse.shape[0], top * (ga // ROW + 1) // 2),
        [VMEM],
        nbytes=2 * top**2,
    )(blocks)
    packed, coming = lax.optimization_barrier((packed, coming))
    packed = lax.all_gather(packed, "ga", axis_index_groups=x_groups)
    for _ in range(chain_rows - 2):
        moved = kernel_call(
            hop_forward, shape(rhs, width), [VMEM] * 4, flops=6 * rhs * width**2
        )(last, coming, ph, plow)
        coming = hop(moved, 1)

    tiles = (ga, rhs * top // ga // 128, 128)
    solved, partial = kernel_call(
        contribute,
        (shape(rhs, width), shape(*tiles)),
        [VMEM] * 7,
        flops=12 * rhs * width**2,
    )(group, coming, qh, ql, across, rows, top_right)
    partial = lax.all_to_all(partial, "ga", 0, 0)
    partial = kernel_call(total_of, shape(gz, *tiles[1:]), [VMEM])(partial)
    partial = lax.all_to_all(partial, "gz", 0, 0)
    partial = kernel_call(total_of, shape(*tiles), [VMEM])(partial)
    partial = lax.all_to_all(partial, "ga", 0, 0)
    partial, packed = lax.optimization_barrier((partial, packed))
    top_solution = kernel_call(
        solve_top,
        shape(rhs, top),
        [VMEM] * 2,
        scratch=[pltpu.VMEM((top, top), BF16), pltpu.VMEM((top, top), BF16)],
        flops=12 * rhs * top**2,
    )(partial, packed)
    reduced = kernel_call(
        lift, shape(ROW, rhs, width), [VMEM] * 4, flops=6 * rhs * top * width
    )(top_solution, across, rows, solved)

    reduced = lax.all_to_all(reduced, "ga", 0, 0, axis_index_groups=x_groups)
    own, sent = kernel_call(
        row_backward,
        (shape(rhs, width), shape(rhs, width)),
        [VMEM] * 3,
        flops=24 * rhs * width**2,
    )(reduced, nh, nl)
    coming = hop(sent, -1)
    for _ in range(chain_rows - 2):
        moved = kernel_call(
            hop_backward, shape(rhs, width), [VMEM] * 4, flops=6 * rhs * width**2
        )(sent, coming, ph, plow)
        coming = hop(moved, -1)
    result = kernel_call(
        finish,
        shape(rhs, width),
        [SMEM] + [VMEM] * 5,
        scratch=[pltpu.VMEM((rhs, width), F32)],
        flops=24 * rhs * width**2,
    )(live_cols, own, coming, nh, nl, inverse)
    return (result[None, None], top_solution)


def solution(mesh):
    placed = (
        P("gz", "ga", None, None),
        P("gz", "ga", None, None),
        P("gz", "ga", None, None),
        P("gz", "ga", None, None),
        P("gz", "ga", None),
        P("gz", "ga"),
        P(),
        P("ga", None),
    )
    return jax.shard_map(
        shards,
        mesh=mesh,
        in_specs=placed,
        out_specs=(P("gz", "ga", None, None), P()),
        check_vma=False,
    )
```

```python
import jax
import jax.numpy as jnp
from jax import lax
from jax.experimental import pallas as pl
from jax.experimental.pallas import tpu as pltpu
from jax.sharding import PartitionSpec as P

BRANCHES = 2
ROW = 4
STORE = 128
NN = (((1,), (0,)), ((), ()))
NT = (((1,), (1,)), ((), ()))
VMEM = pl.BlockSpec(memory_space=pltpu.VMEM)
SMEM = pl.BlockSpec(memory_space=pltpu.SMEM)
HBM = pl.BlockSpec(memory_space=pltpu.HBM)
F32 = jnp.float32
BF16 = jnp.bfloat16


def split(value):
    high = value.astype(BF16)
    return high, (value - high.astype(F32)).astype(BF16)


def bdot(left, right, dims):
    return lax.dot_general(left, right, dims, preferred_element_type=F32)


def dot3(left, right, dims):
    rows = left[0].shape[0]
    both = bdot(jnp.concatenate(left, 0), right[0], dims)
    return both[:rows] + both[rows:] + bdot(left[0], right[1], dims)


def place_in_row():
    return lax.rem(lax.axis_index("ga"), ROW)


def kernel_call(body, outs, ins, scratch=(), flops=0, nbytes=0, limit=16, out_specs=None):
    return pl.pallas_call(
        body,
        out_shape=outs,
        in_specs=ins,
        out_specs=out_specs or jax.tree.map(lambda _: VMEM, outs),
        scratch_shapes=list(scratch),
        compiler_params=pltpu.CompilerParams(vmem_limit_bytes=limit * 2**20),
        cost_estimate=pl.CostEstimate(flops=flops, bytes_accessed=nbytes, transcendentals=0),
    )


def shape(*dims, kind=F32):
    return jax.ShapeDtypeStruct(dims, kind)


def prepare(
    live, right_hbm, inverse_hbm, coupling_hbm, upper_hbm, lower_hbm, right, inverse, coupling, upper, lower, sems
):
    width = inverse.shape[0]
    half = width // 2
    rhs = right.shape[0]
    first, second = pl.ds(0, half), pl.ds(half, half)
    corner = (first, first)
    moves = [
        pltpu.make_async_copy(inverse_hbm.at[corner], inverse.at[corner], sems.at[0]),
        pltpu.make_async_copy(coupling_hbm.at[first], coupling.at[first], sems.at[1]),
        pltpu.make_async_copy(inverse_hbm.at[second], inverse.at[second], sems.at[2]),
        pltpu.make_async_copy(coupling_hbm.at[second], coupling.at[second], sems.at[3]),
        pltpu.make_async_copy(right_hbm, right, sems.at[4]),
    ]
    for move in moves:
        move.start()
    results = [
        pltpu.make_async_copy(upper.at[first], upper_hbm.at[first], sems.at[5]),
        pltpu.make_async_copy(lower.at[first], lower_hbm.at[first], sems.at[6]),
        pltpu.make_async_copy(
            upper.at[pl.ds(half, rhs // 2)], upper_hbm.at[pl.ds(half, rhs // 2)], sems.at[7]
        ),
        pltpu.make_async_copy(
            lower.at[pl.ds(half, rhs // 2)], lower_hbm.at[pl.ds(half, rhs // 2)], sems.at[8]
        ),
    ]
    count = live[0, 0]
    row = lax.broadcasted_iota(jnp.int32, (half, width), 0)
    moves[0].wait()
    corner = split(inverse[:half, :half])
    moves[1].wait()
    ch, cl = split(coupling[:half])
    upper[:half] = jnp.where(row < count, -dot3(corner, (ch, cl), NN), 0.0)
    results[0].start()
    moves[2].wait()
    left = split(inverse[half:, :half])
    bottom = dot3(left, (ch, cl), NN)
    full = split(inverse[half:, half:])
    moves[3].wait()
    bottom = bottom + dot3(full, split(coupling[half:]), NN)
    lower[:half] = jnp.where(row + half < count, -bottom, 0.0)
    results[1].start()
    moves[4].wait()
    sides = split(right[...])
    head, rest = ((sides[0][:, :half], sides[1][:, :half]), (sides[0][:, half:], sides[1][:, half:]))
    own = jnp.concatenate((dot3(head, corner, NT), dot3(head, left, NT) + dot3(rest, full, NT)), 1)
    col = lax.broadcasted_iota(jnp.int32, (rhs, width), 1)
    own = jnp.where(col < count, own, 0.0)
    upper[half:] = own[: rhs // 2]
    lower[half:] = own[rhs // 2 :]
    results[2].start()
    results[3].start()
    for result in results:
        result.wait()


def pack_lower(blocks, out):
    start = 0
    for y in range(blocks.shape[0]):
        wide = (y + 1) * blocks.shape[2] // blocks.shape[0]
        out[:, start : start + wide] = blocks[y, :, :wide]
        start += wide


def place_block(a, b, slot, nh, nl, group):
    half = nh.shape[1] // 2
    rhs = group.shape[1]
    high, low = split(a[:half])
    nh[slot, :half] = high
    nl[slot, :half] = low
    high, low = split(b[:half])
    nh[slot, half:] = high
    nl[slot, half:] = low
    group[slot, : rhs // 2] = a[half:]
    group[slot, rhs // 2 :] = b[half:]


def stage(a0, b0, a1, b1, a3, b3, nh, nl, group):
    for slot, (a, b) in enumerate(((a0, b0), (a1, b1), (a3, b3))):
        place_block(a, b, slot, nh, nl, group)


def assemble(sh, sl, sgroup, a2, b2, nh, nl, group, last):
    here = place_in_row()
    for at, offset in enumerate((0, 1, 3)):
        slot = lax.rem(here + offset, ROW)
        nh[slot] = sh[at]
        nl[slot] = sl[at]
        group[slot] = sgroup[at]
    place_block(a2, b2, lax.rem(here + 2, ROW), nh, nl, group)
    value = group[0]
    for j in range(1, ROW):
        value = group[j] + dot3(split(value), (nh[j], nl[j]), NT)
        group[j] = value
    last[...] = value


def multiply_up(nh, nl, products, store, sems):
    moves = [
        pltpu.make_async_copy(block, store.at[pl.ds(at * ROW, ROW)], sems.at[at])
        for at, block in enumerate((nh, nl))
    ]
    for move in moves:
        move.start()
    here = place_in_row()
    high, low = nh[0], nl[0]

    @pl.when(here == 0)
    def _():
        products[0] = high
        products[1] = low

    for j in range(1, ROW):
        high, low = split(dot3((nh[j], nl[j]), (high, low), NN))

        @pl.when(here == j)
        def _():
            products[0] = high
            products[1] = low

    products[2] = high
    products[3] = low
    for move in moves:
        move.wait()


def hop_forward(base, coming, products, out):
    out[...] = base[...] + dot3(split(coming[...]), (products[2], products[3]), NT)


def hop_backward(base, coming, products, out):
    out[...] = base[...] + dot3(split(coming[...]), (products[2], products[3]), NN)


def onehot_of(rows, top):
    return (lax.broadcasted_iota(jnp.int32, (top, rows.shape[1]), 0) == rows[...]).astype(F32).astype(BF16)


def contribute(group, coming, products, across, rows, top_right, solved, tiles):
    here = place_in_row()
    value = group[here] + dot3(split(coming[...]), (products[0], products[1]), NT)
    solved[...] = value
    pushed = dot3(split(value), split(across[...]), NT)
    count, depth, lanes = tiles.shape
    col_blocks = count * depth // value.shape[0]
    high, low = split(pushed)
    both = bdot(jnp.concatenate((high, low), 0), onehot_of(rows, col_blocks * lanes), NT)
    total = both[: value.shape[0]] + both[value.shape[0] :]
    first = (lax.axis_index("gz") == 0) & (lax.axis_index("ga") == 0)
    total = jnp.where(first, top_right[...] - total, -total)
    for tile in range(count):
        r, c = tile // col_blocks, tile % col_blocks
        tiles[tile] = total[r * depth : (r + 1) * depth, c * lanes : (c + 1) * lanes]


def total_of(pieces, out):
    value = pieces[0]
    for piece in range(1, pieces.shape[0]):
        value = value + pieces[piece]
    for piece in range(out.shape[0]):
        out[piece] = value


def solve_top(tiles, packed, top_out, wh, wl):
    count, depth, lanes = tiles.shape
    rhs, top = top_out.shape
    col_blocks = top // lanes
    steps = packed.shape[1] * packed.shape[0]
    lines = []
    for r in range(rhs // depth):
        lines.append(jnp.concatenate([tiles[r * col_blocks + c] for c in range(col_blocks)], 1))
    rest = split(jnp.concatenate(lines, 0))
    block = 2 * steps
    mid = []
    start = 0
    for step in range(top // steps):
        wide = (step + 1) * steps
        high, low = split(packed[:, :, start : start + wide].reshape(steps, wide))
        at = slice(step * steps, (step + 1) * steps)
        wh[at, :wide] = high
        wl[at, :wide] = low
        start += wide
        if step % 2 == 0:
            wh[at, wide : wide + steps] = jnp.zeros((steps, steps), BF16)
            wl[at, wide : wide + steps] = jnp.zeros((steps, steps), BF16)
        else:
            at = slice(wide - block, wide)
            mid.append(
                dot3((rest[0][:, :wide], rest[1][:, :wide]), (wh[at, :wide], wl[at, :wide]), NT)
            )
    mid = split(jnp.concatenate(mid, 1))
    answer = []
    for j in range(0, top, block):
        end = j + block
        answer.append(
            dot3((mid[0][:, j:], mid[1][:, j:]), (wh[j:, j:end], wl[j:, j:end]), NN)
        )
    top_out[...] = jnp.concatenate(answer, 1)


def lift(top_out, across, rows, solved, reduced):
    rhs, top = top_out.shape
    high, low = split(top_out[...])
    both = bdot(jnp.concatenate((high, low), 0), onehot_of(rows, top), NN)
    lifted = both[:rhs] + both[rhs:]
    value = solved[...] - dot3(split(lifted), split(across[...]), NN)
    for piece in range(reduced.shape[0]):
        reduced[piece] = value


def row_backward(reduced, store, own, sent, nh, nl, sems):
    here = place_in_row()
    moves = [
        [
            pltpu.make_async_copy(store.at[at * ROW + j], block.at[j], sems.at[at, j])
            for at, block in enumerate((nh, nl))
        ]
        for j in range(ROW)
    ]
    for pair_of in reversed(moves):
        for move in pair_of:
            move.start()
    value = reduced[ROW - 1]
    for j in range(ROW - 1, -1, -1):
        if j < ROW - 1:
            value = reduced[j] + value

        @pl.when(here == j)
        def _():
            own[...] = value

        for move in moves[j]:
            move.wait()
        value = dot3(split(value), (nh[j], nl[j]), NN)
    sent[...] = value


def tail(live, own, nh, nl, inverse, settled, zh, zl):
    here = place_in_row()
    row = lax.broadcasted_iota(jnp.int32, inverse.shape, 0)
    high, low = split(jnp.where(row < live[0, 0], inverse[...], 0.0))
    settled[...] = dot3(split(own[...]), (high, low), NN)
    zh[...] = high
    zl[...] = low
    for j in range(1, ROW):

        @pl.when(here < j)
        def _():
            high, low = split(dot3((nh[j], nl[j]), (zh[...], zl[...]), NN))
            zh[...] = high
            zl[...] = low


def finish(settled, coming, zh, zl, out):
    out[...] = settled[...] + dot3(split(coming[...]), (zh[...], zl[...]), NN)


def shards(
    right_sides, diag_inverse, chain_block, top_block, top_rows, live_cols, top_right, top_inverse
):
    ga, gz = lax.axis_size("ga"), lax.axis_size("gz")
    chain_len = ga // BRANCHES
    chain_rows = chain_len // ROW
    right, inverse = right_sides[0, 0], diag_inverse[0, 0]
    coupling, across = chain_block[0, 0], top_block[0, 0]
    rows = top_rows[0]
    rhs, width = right.shape
    top = top_right.shape[1]
    x_groups = [[r * ROW + c for c in range(ROW)] for r in range(ga // ROW)]
    y_groups = [[r * ROW + c for r in range(ga // ROW)] for c in range(ROW)]

    def ring(value, step):
        return lax.ppermute(
            value, "ga", [(i, i // ROW * ROW + (i + step) % ROW) for i in range(ga)]
        )

    def hop(value, step):
        route = [
            (i, i + step * ROW)
            for i in range(ga)
            if 0 <= i // ROW % chain_rows + step < chain_rows
        ]
        return lax.ppermute(value, "ga", route)

    def pair(*dims):
        return (shape(*dims, kind=BF16), shape(*dims, kind=BF16))

    half = width // 2 + rhs // 2
    a0, b0 = kernel_call(
        prepare,
        (shape(half, width), shape(half, width)),
        [SMEM, HBM, HBM, HBM],
        scratch=[
            pltpu.VMEM((rhs, width), F32),
            pltpu.VMEM((width, width), F32),
            pltpu.VMEM((width, width), F32),
            pltpu.VMEM((half, width), F32),
            pltpu.VMEM((half, width), F32),
            pltpu.SemaphoreType.DMA((9,)),
        ],
        out_specs=(HBM, HBM),
        flops=6 * width**3,
        nbytes=16 * width**2,
        limit=60,
    )(live_cols, right, inverse, coupling)
    top_inverse, a0 = lax.optimization_barrier((top_inverse, a0))
    blocks = lax.all_gather(top_inverse, "ga", axis_index_groups=y_groups)
    a3 = ring(a0, 1)
    b1 = ring(b0, -1)
    b3 = ring(b0, 1)
    a1 = ring(a0, -1)
    a2 = ring(a3, 1)
    b2 = ring(b1, -1)

    staged = kernel_call(
        stage,
        pair(ROW - 1, width, width) + (shape(ROW - 1, rhs, width),),
        [VMEM] * 6,
        nbytes=32 * width**2,
    )(a0, b0, a1, b1, a3, b3)
    nh, nl, group, last = kernel_call(
        assemble,
        pair(ROW, width, width) + (shape(ROW, rhs, width), shape(rhs, width)),
        [VMEM] * 5,
        flops=24 * rhs * width**2,
        nbytes=32 * width**2,
    )(*staged, a2, b2)
    coming = hop(last, 1)
    products, store = kernel_call(
        multiply_up,
        (shape(4, width, width, kind=BF16), shape(STORE, width, width, kind=BF16)),
        [VMEM, VMEM],
        scratch=[pltpu.SemaphoreType.DMA((2,))],
        out_specs=(VMEM, HBM),
        flops=18 * width**3,
        nbytes=24 * width**2,
    )(nh, nl)
    blocks, coming, products = lax.optimization_barrier((blocks, coming, products))
    packed = kernel_call(
        pack_lower,
        shape(top_inverse.shape[0], top * (ga // ROW + 1) // 2),
        [VMEM],
        nbytes=2 * top**2,
    )(blocks)
    for step in range(chain_rows - 2):
        moved = kernel_call(
            hop_forward, shape(rhs, width), [VMEM] * 3, flops=6 * rhs * width**2
        )(last, coming, products)
        coming = hop(moved, 1)
        if step == 0:
            packed, coming = lax.optimization_barrier((packed, coming))
    packed = lax.all_gather(packed, "ga", axis_index_groups=x_groups)

    tiles = (ga, rhs * top // ga // 128, 128)
    solved, partial = kernel_call(
        contribute,
        (shape(rhs, width), shape(*tiles)),
        [VMEM] * 6,
        flops=12 * rhs * width**2,
    )(group, coming, products, across, rows, top_right)
    partial = lax.all_to_all(partial, "ga", 0, 0)
    partial = kernel_call(total_of, shape(gz, *tiles[1:]), [VMEM])(partial)
    partial = lax.all_to_all(partial, "gz", 0, 0)
    partial = kernel_call(total_of, shape(*tiles), [VMEM])(partial)
    partial = lax.all_to_all(partial, "ga", 0, 0)
    partial, packed = lax.optimization_barrier((partial, packed))
    top_solution = kernel_call(
        solve_top,
        shape(rhs, top),
        [VMEM] * 2,
        scratch=[pltpu.VMEM((top, top), BF16), pltpu.VMEM((top, top), BF16)],
        flops=12 * rhs * top**2,
    )(partial, packed)
    reduced = kernel_call(
        lift, shape(ROW, rhs, width), [VMEM] * 4, flops=6 * rhs * top * width
    )(top_solution, across, rows, solved)

    reduced = lax.all_to_all(reduced, "ga", 0, 0, axis_index_groups=x_groups)
    own, sent, nh, nl = kernel_call(
        row_backward,
        (shape(rhs, width), shape(rhs, width)) + pair(ROW, width, width),
        [VMEM, HBM],
        scratch=[pltpu.SemaphoreType.DMA((2, ROW))],
        flops=24 * rhs * width**2,
    )(reduced, store)
    coming = hop(sent, -1)
    settled, zh, zl = kernel_call(
        tail,
        (shape(rhs, width),) + pair(width, width),
        [SMEM] + [VMEM] * 4,
        flops=18 * width**3,
        nbytes=24 * width**2,
    )(live_cols, own, nh, nl, inverse)
    for _ in range(chain_rows - 2):
        moved = kernel_call(
            hop_backward, shape(rhs, width), [VMEM] * 3, flops=6 * rhs * width**2
        )(sent, coming, products)
        coming = hop(moved, -1)
    result = kernel_call(
        finish, shape(rhs, width), [VMEM] * 4, flops=6 * rhs * width**2
    )(settled, coming, zh, zl)
    return (result[None, None], top_solution)


def solution(mesh):
    placed = (
        P("gz", "ga", None, None),
        P("gz", "ga", None, None),
        P("gz", "ga", None, None),
        P("gz", "ga", None, None),
        P("gz", "ga", None),
        P("gz", "ga"),
        P(),
        P("ga", None),
    )
    return jax.shard_map(
        shards,
        mesh=mesh,
        in_specs=placed,
        out_specs=(P("gz", "ga", None, None), P()),
        check_vma=False,
    )
```

```python
import jax
import jax.numpy as jnp
from jax import lax
from jax.experimental import pallas as pl
from jax.experimental.pallas import tpu as pltpu
from jax.sharding import PartitionSpec as P

BRANCHES = 2
ROW = 4
STORE = 128
NN = (((1,), (0,)), ((), ()))
NT = (((1,), (1,)), ((), ()))
VMEM = pl.BlockSpec(memory_space=pltpu.VMEM)
SMEM = pl.BlockSpec(memory_space=pltpu.SMEM)
HBM = pl.BlockSpec(memory_space=pltpu.HBM)
F32 = jnp.float32
BF16 = jnp.bfloat16


def split(value):
    high = value.astype(BF16)
    return high, (value - high.astype(F32)).astype(BF16)


def bdot(left, right, dims):
    return lax.dot_general(left, right, dims, preferred_element_type=F32)


def dot3(left, right, dims):
    rows = left[0].shape[0]
    both = bdot(jnp.concatenate(left, 0), right[0], dims)
    return both[:rows] + both[rows:] + bdot(left[0], right[1], dims)


def place_in_row():
    return lax.rem(lax.axis_index("ga"), ROW)


def kernel_call(body, outs, ins, scratch=(), flops=0, nbytes=0, limit=16, out_specs=None):
    return pl.pallas_call(
        body,
        out_shape=outs,
        in_specs=ins,
        out_specs=out_specs or jax.tree.map(lambda _: VMEM, outs),
        scratch_shapes=list(scratch),
        compiler_params=pltpu.CompilerParams(vmem_limit_bytes=limit * 2**20),
        cost_estimate=pl.CostEstimate(flops=flops, bytes_accessed=nbytes, transcendentals=0),
    )


def shape(*dims, kind=F32):
    return jax.ShapeDtypeStruct(dims, kind)


def prepare(
    live, right_hbm, inverse_hbm, coupling_hbm, upper_hbm, lower_hbm, right, inverse, coupling, upper, lower, sems
):
    width = inverse.shape[0]
    half = width // 2
    rhs = right.shape[0]
    first, second = pl.ds(0, half), pl.ds(half, half)
    corner = (first, first)
    moves = [
        pltpu.make_async_copy(inverse_hbm.at[corner], inverse.at[corner], sems.at[0]),
        pltpu.make_async_copy(coupling_hbm.at[first], coupling.at[first], sems.at[1]),
        pltpu.make_async_copy(inverse_hbm.at[second], inverse.at[second], sems.at[2]),
        pltpu.make_async_copy(coupling_hbm.at[second], coupling.at[second], sems.at[3]),
        pltpu.make_async_copy(right_hbm, right, sems.at[4]),
    ]
    for move in moves:
        move.start()
    results = [
        pltpu.make_async_copy(upper.at[first], upper_hbm.at[first], sems.at[5]),
        pltpu.make_async_copy(lower.at[first], lower_hbm.at[first], sems.at[6]),
        pltpu.make_async_copy(
            upper.at[pl.ds(half, rhs // 2)], upper_hbm.at[pl.ds(half, rhs // 2)], sems.at[7]
        ),
        pltpu.make_async_copy(
            lower.at[pl.ds(half, rhs // 2)], lower_hbm.at[pl.ds(half, rhs // 2)], sems.at[8]
        ),
    ]
    count = live[0, 0]
    row = lax.broadcasted_iota(jnp.int32, (half, width), 0)
    moves[0].wait()
    corner = split(inverse[:half, :half])
    moves[1].wait()
    ch, cl = split(coupling[:half])
    upper[:half] = jnp.where(row < count, -dot3(corner, (ch, cl), NN), 0.0)
    results[0].start()
    moves[2].wait()
    left = split(inverse[half:, :half])
    bottom = dot3(left, (ch, cl), NN)
    full = split(inverse[half:, half:])
    moves[3].wait()
    bottom = bottom + dot3(full, split(coupling[half:]), NN)
    lower[:half] = jnp.where(row + half < count, -bottom, 0.0)
    results[1].start()
    moves[4].wait()
    sides = split(right[...])
    head, rest = ((sides[0][:, :half], sides[1][:, :half]), (sides[0][:, half:], sides[1][:, half:]))
    own = jnp.concatenate((dot3(head, corner, NT), dot3(head, left, NT) + dot3(rest, full, NT)), 1)
    col = lax.broadcasted_iota(jnp.int32, (rhs, width), 1)
    own = jnp.where(col < count, own, 0.0)
    upper[half:] = own[: rhs // 2]
    lower[half:] = own[rhs // 2 :]
    results[2].start()
    results[3].start()
    for result in results:
        result.wait()


def pack_lower(blocks, out):
    start = 0
    for y in range(blocks.shape[0]):
        wide = (y + 1) * blocks.shape[2] // blocks.shape[0]
        out[:, start : start + wide] = blocks[y, :, :wide]
        start += wide


def place_block(a, b, slot, nh, nl, group):
    half = nh.shape[1] // 2
    rhs = group.shape[1]
    high, low = split(a[:half])
    nh[slot, :half] = high
    nl[slot, :half] = low
    high, low = split(b[:half])
    nh[slot, half:] = high
    nl[slot, half:] = low
    group[slot, : rhs // 2] = a[half:]
    group[slot, rhs // 2 :] = b[half:]


def stage(a0, b0, a1, b1, a3, b3, nh, nl, group):
    for slot, (a, b) in enumerate(((a0, b0), (a1, b1), (a3, b3))):
        place_block(a, b, slot, nh, nl, group)


def assemble(sh, sl, sgroup, a2, b2, nh, nl, group, last):
    here = place_in_row()
    for at, offset in enumerate((0, 1, 3)):
        slot = lax.rem(here + offset, ROW)
        nh[slot] = sh[at]
        nl[slot] = sl[at]
        group[slot] = sgroup[at]
    place_block(a2, b2, lax.rem(here + 2, ROW), nh, nl, group)
    value = group[0]
    for j in range(1, ROW):
        value = group[j] + dot3(split(value), (nh[j], nl[j]), NT)
        group[j] = value
    last[...] = value


def multiply_up(nh, nl, products, store, sems):
    moves = [
        pltpu.make_async_copy(block, store.at[pl.ds(at * ROW, ROW)], sems.at[at])
        for at, block in enumerate((nh, nl))
    ]
    for move in moves:
        move.start()
    here = place_in_row()
    high, low = nh[0], nl[0]

    @pl.when(here == 0)
    def _():
        products[0] = high
        products[1] = low

    for j in range(1, ROW):
        high, low = split(dot3((nh[j], nl[j]), (high, low), NN))

        @pl.when(here == j)
        def _():
            products[0] = high
            products[1] = low

    products[2] = high
    products[3] = low
    for move in moves:
        move.wait()


def hop_forward(base, coming, products, out):
    out[...] = base[...] + dot3(split(coming[...]), (products[2], products[3]), NT)


def hop_backward(base, coming, products, out):
    out[...] = base[...] + dot3(split(coming[...]), (products[2], products[3]), NN)


def onehot_of(rows, top):
    return (lax.broadcasted_iota(jnp.int32, (top, rows.shape[1]), 0) == rows[...]).astype(F32).astype(BF16)


def contribute(group, coming, products, across, rows, top_right, solved, tiles):
    here = place_in_row()
    value = group[here] + dot3(split(coming[...]), (products[0], products[1]), NT)
    solved[...] = value
    pushed = dot3(split(value), split(across[...]), NT)
    count, depth, lanes = tiles.shape
    col_blocks = count * depth // value.shape[0]
    high, low = split(pushed)
    both = bdot(jnp.concatenate((high, low), 0), onehot_of(rows, col_blocks * lanes), NT)
    total = both[: value.shape[0]] + both[value.shape[0] :]
    first = (lax.axis_index("gz") == 0) & (lax.axis_index("ga") == 0)
    total = jnp.where(first, top_right[...] - total, -total)
    for tile in range(count):
        r, c = tile // col_blocks, tile % col_blocks
        tiles[tile] = total[r * depth : (r + 1) * depth, c * lanes : (c + 1) * lanes]


def total_of(pieces, out):
    value = pieces[0]
    for piece in range(1, pieces.shape[0]):
        value = value + pieces[piece]
    for piece in range(out.shape[0]):
        out[piece] = value


def solve_top(tiles, packed, store, top_out, nh, nl, wh, wl, sems):
    count, depth, lanes = tiles.shape
    rhs, top = top_out.shape
    col_blocks = top // lanes
    steps = packed.shape[1] * packed.shape[0]
    moves = [
        pltpu.make_async_copy(store.at[pl.ds(at * ROW, ROW)], block, sems.at[at])
        for at, block in enumerate((nh, nl))
    ]
    for move in moves:
        move.start()
    lines = []
    for r in range(rhs // depth):
        lines.append(jnp.concatenate([tiles[r * col_blocks + c] for c in range(col_blocks)], 1))
    rest = split(jnp.concatenate(lines, 0))
    block = 2 * steps
    mid = []
    start = 0
    for step in range(top // steps):
        wide = (step + 1) * steps
        high, low = split(packed[:, :, start : start + wide].reshape(steps, wide))
        at = slice(step * steps, (step + 1) * steps)
        wh[at, :wide] = high
        wl[at, :wide] = low
        start += wide
        if step % 2 == 0:
            wh[at, wide : wide + steps] = jnp.zeros((steps, steps), BF16)
            wl[at, wide : wide + steps] = jnp.zeros((steps, steps), BF16)
        else:
            at = slice(wide - block, wide)
            mid.append(
                dot3((rest[0][:, :wide], rest[1][:, :wide]), (wh[at, :wide], wl[at, :wide]), NT)
            )
    mid = split(jnp.concatenate(mid, 1))
    answer = []
    for j in range(0, top, block):
        end = j + block
        answer.append(
            dot3((mid[0][:, j:], mid[1][:, j:]), (wh[j:, j:end], wl[j:, j:end]), NN)
        )
    top_out[...] = jnp.concatenate(answer, 1)
    for move in moves:
        move.wait()


def lift(top_out, across, rows, solved, reduced):
    rhs, top = top_out.shape
    high, low = split(top_out[...])
    both = bdot(jnp.concatenate((high, low), 0), onehot_of(rows, top), NN)
    lifted = both[:rhs] + both[rhs:]
    value = solved[...] - dot3(split(lifted), split(across[...]), NN)
    for piece in range(reduced.shape[0]):
        reduced[piece] = value


def row_backward(reduced, nh, nl, own, sent):
    here = place_in_row()
    value = reduced[ROW - 1]
    for j in range(ROW - 1, -1, -1):
        if j < ROW - 1:
            value = reduced[j] + value

        @pl.when(here == j)
        def _():
            own[...] = value

        value = dot3(split(value), (nh[j], nl[j]), NN)
    sent[...] = value


def tail(live, own, nh, nl, inverse, settled, zh, zl):
    here = place_in_row()
    row = lax.broadcasted_iota(jnp.int32, inverse.shape, 0)
    high, low = split(jnp.where(row < live[0, 0], inverse[...], 0.0))
    settled[...] = dot3(split(own[...]), (high, low), NN)
    zh[...] = high
    zl[...] = low
    for j in range(1, ROW):

        @pl.when(here < j)
        def _():
            high, low = split(dot3((nh[j], nl[j]), (zh[...], zl[...]), NN))
            zh[...] = high
            zl[...] = low


def finish(settled, coming, zh, zl, out):
    out[...] = settled[...] + dot3(split(coming[...]), (zh[...], zl[...]), NN)


def shards(
    right_sides, diag_inverse, chain_block, top_block, top_rows, live_cols, top_right, top_inverse
):
    ga, gz = lax.axis_size("ga"), lax.axis_size("gz")
    chain_len = ga // BRANCHES
    chain_rows = chain_len // ROW
    right, inverse = right_sides[0, 0], diag_inverse[0, 0]
    coupling, across = chain_block[0, 0], top_block[0, 0]
    rows = top_rows[0]
    rhs, width = right.shape
    top = top_right.shape[1]
    x_groups = [[r * ROW + c for c in range(ROW)] for r in range(ga // ROW)]
    y_groups = [[r * ROW + c for r in range(ga // ROW)] for c in range(ROW)]

    def ring(value, step):
        return lax.ppermute(
            value, "ga", [(i, i // ROW * ROW + (i + step) % ROW) for i in range(ga)]
        )

    def hop(value, step):
        route = [
            (i, i + step * ROW)
            for i in range(ga)
            if 0 <= i // ROW % chain_rows + step < chain_rows
        ]
        return lax.ppermute(value, "ga", route)

    def pair(*dims):
        return (shape(*dims, kind=BF16), shape(*dims, kind=BF16))

    half = width // 2 + rhs // 2
    a0, b0 = kernel_call(
        prepare,
        (shape(half, width), shape(half, width)),
        [SMEM, HBM, HBM, HBM],
        scratch=[
            pltpu.VMEM((rhs, width), F32),
            pltpu.VMEM((width, width), F32),
            pltpu.VMEM((width, width), F32),
            pltpu.VMEM((half, width), F32),
            pltpu.VMEM((half, width), F32),
            pltpu.SemaphoreType.DMA((9,)),
        ],
        out_specs=(HBM, HBM),
        flops=6 * width**3,
        nbytes=16 * width**2,
        limit=60,
    )(live_cols, right, inverse, coupling)
    top_inverse, a0 = lax.optimization_barrier((top_inverse, a0))
    blocks = lax.all_gather(top_inverse, "ga", axis_index_groups=y_groups)
    a3 = ring(a0, 1)
    b1 = ring(b0, -1)
    b3 = ring(b0, 1)
    a1 = ring(a0, -1)
    a2 = ring(a3, 1)
    b2 = ring(b1, -1)

    staged = kernel_call(
        stage,
        pair(ROW - 1, width, width) + (shape(ROW - 1, rhs, width),),
        [VMEM] * 6,
        nbytes=32 * width**2,
    )(a0, b0, a1, b1, a3, b3)
    nh, nl, group, last = kernel_call(
        assemble,
        pair(ROW, width, width) + (shape(ROW, rhs, width), shape(rhs, width)),
        [VMEM] * 5,
        flops=24 * rhs * width**2,
        nbytes=32 * width**2,
    )(*staged, a2, b2)
    coming = hop(last, 1)
    products, store = kernel_call(
        multiply_up,
        (shape(4, width, width, kind=BF16), shape(STORE, width, width, kind=BF16)),
        [VMEM, VMEM],
        scratch=[pltpu.SemaphoreType.DMA((2,))],
        out_specs=(VMEM, HBM),
        flops=18 * width**3,
        nbytes=24 * width**2,
    )(nh, nl)
    blocks, coming, products = lax.optimization_barrier((blocks, coming, products))
    packed = kernel_call(
        pack_lower,
        shape(top_inverse.shape[0], top * (ga // ROW + 1) // 2),
        [VMEM],
        nbytes=2 * top**2,
    )(blocks)
    for step in range(chain_rows - 2):
        moved = kernel_call(
            hop_forward, shape(rhs, width), [VMEM] * 3, flops=6 * rhs * width**2
        )(last, coming, products)
        coming = hop(moved, 1)
        if step == 0:
            packed, coming = lax.optimization_barrier((packed, coming))
    packed = lax.all_gather(packed, "ga", axis_index_groups=x_groups)

    tiles = (ga, rhs * top // ga // 128, 128)
    solved, partial = kernel_call(
        contribute,
        (shape(rhs, width), shape(*tiles)),
        [VMEM] * 6,
        flops=12 * rhs * width**2,
    )(group, coming, products, across, rows, top_right)
    partial = lax.all_to_all(partial, "ga", 0, 0)
    partial = kernel_call(total_of, shape(gz, *tiles[1:]), [VMEM])(partial)
    partial = lax.all_to_all(partial, "gz", 0, 0)
    partial = kernel_call(total_of, shape(*tiles), [VMEM])(partial)
    partial = lax.all_to_all(partial, "ga", 0, 0)
    partial, packed = lax.optimization_barrier((partial, packed))
    top_solution, nh, nl = kernel_call(
        solve_top,
        (shape(rhs, top),) + pair(ROW, width, width),
        [VMEM, VMEM, HBM],
        scratch=[
            pltpu.VMEM((top, top), BF16),
            pltpu.VMEM((top, top), BF16),
            pltpu.SemaphoreType.DMA((2,)),
        ],
        flops=12 * rhs * top**2,
    )(partial, packed, store)
    reduced = kernel_call(
        lift, shape(ROW, rhs, width), [VMEM] * 4, flops=6 * rhs * top * width
    )(top_solution, across, rows, solved)

    reduced = lax.all_to_all(reduced, "ga", 0, 0, axis_index_groups=x_groups)
    own, sent = kernel_call(
        row_backward,
        (shape(rhs, width), shape(rhs, width)),
        [VMEM] * 3,
        flops=24 * rhs * width**2,
    )(reduced, nh, nl)
    coming = hop(sent, -1)
    settled, zh, zl = kernel_call(
        tail,
        (shape(rhs, width),) + pair(width, width),
        [SMEM] + [VMEM] * 4,
        flops=18 * width**3,
        nbytes=24 * width**2,
    )(live_cols, own, nh, nl, inverse)
    for _ in range(chain_rows - 2):
        moved = kernel_call(
            hop_backward, shape(rhs, width), [VMEM] * 3, flops=6 * rhs * width**2
        )(sent, coming, products)
        coming = hop(moved, -1)
    result = kernel_call(
        finish, shape(rhs, width), [VMEM] * 4, flops=6 * rhs * width**2
    )(settled, coming, zh, zl)
    return (result[None, None], top_solution)


def solution(mesh):
    placed = (
        P("gz", "ga", None, None),
        P("gz", "ga", None, None),
        P("gz", "ga", None, None),
        P("gz", "ga", None, None),
        P("gz", "ga", None),
        P("gz", "ga"),
        P(),
        P("ga", None),
    )
    return jax.shard_map(
        shards,
        mesh=mesh,
        in_specs=placed,
        out_specs=(P("gz", "ga", None, None), P()),
        check_vma=False,
    )
```

```python
import jax
import jax.numpy as jnp
from jax import lax
from jax.experimental import pallas as pl
from jax.experimental.pallas import tpu as pltpu
from jax.sharding import PartitionSpec as P

BRANCHES = 2
ROW = 4
STORE = 128
NN = (((1,), (0,)), ((), ()))
NT = (((1,), (1,)), ((), ()))
VMEM = pl.BlockSpec(memory_space=pltpu.VMEM)
SMEM = pl.BlockSpec(memory_space=pltpu.SMEM)
HBM = pl.BlockSpec(memory_space=pltpu.HBM)
F32 = jnp.float32
BF16 = jnp.bfloat16


def split(value):
    high = value.astype(BF16)
    return high, (value - high.astype(F32)).astype(BF16)


def bdot(left, right, dims):
    return lax.dot_general(left, right, dims, preferred_element_type=F32)


def dot3(left, right, dims):
    rows = left[0].shape[0]
    both = bdot(jnp.concatenate(left, 0), right[0], dims)
    return both[:rows] + both[rows:] + bdot(left[0], right[1], dims)


def place_in_row():
    return lax.rem(lax.axis_index("ga"), ROW)


def kernel_call(body, outs, ins, scratch=(), flops=0, nbytes=0, limit=16, out_specs=None):
    return pl.pallas_call(
        body,
        out_shape=outs,
        in_specs=ins,
        out_specs=out_specs or jax.tree.map(lambda _: VMEM, outs),
        scratch_shapes=list(scratch),
        compiler_params=pltpu.CompilerParams(vmem_limit_bytes=limit * 2**20),
        cost_estimate=pl.CostEstimate(flops=flops, bytes_accessed=nbytes, transcendentals=0),
    )


def shape(*dims, kind=F32):
    return jax.ShapeDtypeStruct(dims, kind)


def prepare(
    live, right_hbm, inverse_hbm, coupling_hbm, upper_hbm, lower_hbm, right, inverse, coupling, upper, lower, sems
):
    width = inverse.shape[0]
    half = width // 2
    rhs = right.shape[0]
    first, second = pl.ds(0, half), pl.ds(half, half)
    corner = (first, first)
    moves = [
        pltpu.make_async_copy(inverse_hbm.at[corner], inverse.at[corner], sems.at[0]),
        pltpu.make_async_copy(coupling_hbm.at[first], coupling.at[first], sems.at[1]),
        pltpu.make_async_copy(inverse_hbm.at[second], inverse.at[second], sems.at[2]),
        pltpu.make_async_copy(coupling_hbm.at[second], coupling.at[second], sems.at[3]),
        pltpu.make_async_copy(right_hbm, right, sems.at[4]),
    ]
    for move in moves:
        move.start()
    results = [
        pltpu.make_async_copy(upper.at[first], upper_hbm.at[first], sems.at[5]),
        pltpu.make_async_copy(lower.at[first], lower_hbm.at[first], sems.at[6]),
        pltpu.make_async_copy(
            upper.at[pl.ds(half, rhs // 2)], upper_hbm.at[pl.ds(half, rhs // 2)], sems.at[7]
        ),
        pltpu.make_async_copy(
            lower.at[pl.ds(half, rhs // 2)], lower_hbm.at[pl.ds(half, rhs // 2)], sems.at[8]
        ),
    ]
    count = live[0, 0]
    row = lax.broadcasted_iota(jnp.int32, (half, width), 0)
    moves[0].wait()
    corner = split(inverse[:half, :half])
    moves[1].wait()
    ch, cl = split(coupling[:half])
    upper[:half] = jnp.where(row < count, -dot3(corner, (ch, cl), NN), 0.0)
    results[0].start()
    moves[2].wait()
    left = split(inverse[half:, :half])
    bottom = dot3(left, (ch, cl), NN)
    full = split(inverse[half:, half:])
    moves[3].wait()
    bottom = bottom + dot3(full, split(coupling[half:]), NN)
    lower[:half] = jnp.where(row + half < count, -bottom, 0.0)
    results[1].start()
    moves[4].wait()
    sides = split(right[...])
    head, rest = ((sides[0][:, :half], sides[1][:, :half]), (sides[0][:, half:], sides[1][:, half:]))
    own = jnp.concatenate((dot3(head, corner, NT), dot3(head, left, NT) + dot3(rest, full, NT)), 1)
    col = lax.broadcasted_iota(jnp.int32, (rhs, width), 1)
    own = jnp.where(col < count, own, 0.0)
    upper[half:] = own[: rhs // 2]
    lower[half:] = own[rhs // 2 :]
    results[2].start()
    results[3].start()
    for result in results:
        result.wait()


def pack_lower(blocks, out):
    start = 0
    for y in range(blocks.shape[0]):
        wide = (y + 1) * blocks.shape[2] // blocks.shape[0]
        out[:, start : start + wide] = blocks[y, :, :wide]
        start += wide


def place_block(a, b, slot, nh, nl, group):
    half = nh.shape[1] // 2
    rhs = group.shape[1]
    high, low = split(a[:half])
    nh[slot, :half] = high
    nl[slot, :half] = low
    high, low = split(b[:half])
    nh[slot, half:] = high
    nl[slot, half:] = low
    group[slot, : rhs // 2] = a[half:]
    group[slot, rhs // 2 :] = b[half:]


def stage(a0, b0, a1, b1, a3, b3, nh, nl, group):
    for slot, (a, b) in enumerate(((a0, b0), (a1, b1), (a3, b3))):
        place_block(a, b, slot, nh, nl, group)


def assemble(sh, sl, sgroup, a2, b2, nh, nl, group, last):
    here = place_in_row()
    for at, offset in enumerate((0, 1, 3)):
        slot = lax.rem(here + offset, ROW)
        nh[slot] = sh[at]
        nl[slot] = sl[at]
        group[slot] = sgroup[at]
    place_block(a2, b2, lax.rem(here + 2, ROW), nh, nl, group)
    value = group[0]
    for j in range(1, ROW):
        value = group[j] + dot3(split(value), (nh[j], nl[j]), NT)
        group[j] = value
    last[...] = value


def multiply_up(nh, nl, products, store, sems):
    moves = [
        pltpu.make_async_copy(block, store.at[pl.ds(at * ROW, ROW)], sems.at[at])
        for at, block in enumerate((nh, nl))
    ]
    for move in moves:
        move.start()
    here = place_in_row()
    high, low = nh[0], nl[0]

    @pl.when(here == 0)
    def _():
        products[0] = high
        products[1] = low

    for j in range(1, ROW):
        high, low = split(dot3((nh[j], nl[j]), (high, low), NN))

        @pl.when(here == j)
        def _():
            products[0] = high
            products[1] = low

    products[2] = high
    products[3] = low
    for move in moves:
        move.wait()


def hop_forward(base, coming, products, out):
    out[...] = base[...] + dot3(split(coming[...]), (products[2], products[3]), NT)


def hop_backward(base, coming, products, out):
    out[...] = base[...] + dot3(split(coming[...]), (products[2], products[3]), NN)


def onehot_of(rows, top):
    return (lax.broadcasted_iota(jnp.int32, (top, rows.shape[1]), 0) == rows[...]).astype(F32).astype(BF16)


def contribute(group, products, across, rows, top_right, *others):
    *came, solved, tiles = others
    here = place_in_row()
    coming = sum(block[...] for block in came)
    value = group[here] + dot3(split(coming), (products[0], products[1]), NT)
    solved[...] = value
    pushed = dot3(split(value), split(across[...]), NT)
    count, depth, lanes = tiles.shape
    col_blocks = count * depth // value.shape[0]
    high, low = split(pushed)
    both = bdot(jnp.concatenate((high, low), 0), onehot_of(rows, col_blocks * lanes), NT)
    total = both[: value.shape[0]] + both[value.shape[0] :]
    first = (lax.axis_index("gz") == 0) & (lax.axis_index("ga") == 0)
    total = jnp.where(first, top_right[...] - total, -total)
    for tile in range(count):
        r, c = tile // col_blocks, tile % col_blocks
        tiles[tile] = total[r * depth : (r + 1) * depth, c * lanes : (c + 1) * lanes]


def total_of(pieces, out):
    value = pieces[0]
    for piece in range(1, pieces.shape[0]):
        value = value + pieces[piece]
    for piece in range(out.shape[0]):
        out[piece] = value


def solve_top(tiles, packed, store, top_out, nh, nl, wh, wl, sems):
    count, depth, lanes = tiles.shape
    rhs, top = top_out.shape
    col_blocks = top // lanes
    steps = packed.shape[1] * packed.shape[0]
    moves = [
        pltpu.make_async_copy(store.at[pl.ds(at * ROW, ROW)], block, sems.at[at])
        for at, block in enumerate((nh, nl))
    ]
    for move in moves:
        move.start()
    lines = []
    for r in range(rhs // depth):
        lines.append(jnp.concatenate([tiles[r * col_blocks + c] for c in range(col_blocks)], 1))
    rest = split(jnp.concatenate(lines, 0))
    block = 2 * steps
    mid = []
    start = 0
    for step in range(top // steps):
        wide = (step + 1) * steps
        high, low = split(packed[:, :, start : start + wide].reshape(steps, wide))
        at = slice(step * steps, (step + 1) * steps)
        wh[at, :wide] = high
        wl[at, :wide] = low
        start += wide
        if step % 2 == 0:
            wh[at, wide : wide + steps] = jnp.zeros((steps, steps), BF16)
            wl[at, wide : wide + steps] = jnp.zeros((steps, steps), BF16)
        else:
            at = slice(wide - block, wide)
            mid.append(
                dot3((rest[0][:, :wide], rest[1][:, :wide]), (wh[at, :wide], wl[at, :wide]), NT)
            )
    mid = split(jnp.concatenate(mid, 1))
    answer = []
    for j in range(0, top, block):
        end = j + block
        answer.append(
            dot3((mid[0][:, j:], mid[1][:, j:]), (wh[j:, j:end], wl[j:, j:end]), NN)
        )
    top_out[...] = jnp.concatenate(answer, 1)
    for move in moves:
        move.wait()


def lift(top_out, across, rows, solved, reduced):
    rhs, top = top_out.shape
    high, low = split(top_out[...])
    both = bdot(jnp.concatenate((high, low), 0), onehot_of(rows, top), NN)
    lifted = both[:rhs] + both[rhs:]
    value = solved[...] - dot3(split(lifted), split(across[...]), NN)
    for piece in range(reduced.shape[0]):
        reduced[piece] = value


def row_backward(reduced, nh, nl, own, sent):
    here = place_in_row()
    value = reduced[ROW - 1]
    for j in range(ROW - 1, -1, -1):
        if j < ROW - 1:
            value = reduced[j] + value

        @pl.when(here == j)
        def _():
            own[...] = value

        value = dot3(split(value), (nh[j], nl[j]), NN)
    sent[...] = value


def tail(live, own, nh, nl, inverse, settled, zh, zl):
    here = place_in_row()
    row = lax.broadcasted_iota(jnp.int32, inverse.shape, 0)
    high, low = split(jnp.where(row < live[0, 0], inverse[...], 0.0))
    settled[...] = dot3(split(own[...]), (high, low), NN)
    zh[...] = high
    zl[...] = low
    for j in range(1, ROW):

        @pl.when(here < j)
        def _():
            high, low = split(dot3((nh[j], nl[j]), (zh[...], zl[...]), NN))
            zh[...] = high
            zl[...] = low


def finish(settled, zh, zl, *others):
    *came, out = others
    coming = sum(block[...] for block in came)
    out[...] = settled[...] + dot3(split(coming), (zh[...], zl[...]), NN)


def shards(
    right_sides, diag_inverse, chain_block, top_block, top_rows, live_cols, top_right, top_inverse
):
    ga, gz = lax.axis_size("ga"), lax.axis_size("gz")
    chain_len = ga // BRANCHES
    chain_rows = chain_len // ROW
    right, inverse = right_sides[0, 0], diag_inverse[0, 0]
    coupling, across = chain_block[0, 0], top_block[0, 0]
    rows = top_rows[0]
    rhs, width = right.shape
    top = top_right.shape[1]
    x_groups = [[r * ROW + c for c in range(ROW)] for r in range(ga // ROW)]
    y_groups = [[r * ROW + c for r in range(ga // ROW)] for c in range(ROW)]

    def ring(value, step):
        return lax.ppermute(
            value, "ga", [(i, i // ROW * ROW + (i + step) % ROW) for i in range(ga)]
        )

    def hop(value, row, step):
        route = [(i, i + step * ROW) for i in range(ga) if i // ROW % chain_rows == row]
        return lax.ppermute(value, "ga", route)

    def pair(*dims):
        return (shape(*dims, kind=BF16), shape(*dims, kind=BF16))

    half = width // 2 + rhs // 2
    a0, b0 = kernel_call(
        prepare,
        (shape(half, width), shape(half, width)),
        [SMEM, HBM, HBM, HBM],
        scratch=[
            pltpu.VMEM((rhs, width), F32),
            pltpu.VMEM((width, width), F32),
            pltpu.VMEM((width, width), F32),
            pltpu.VMEM((half, width), F32),
            pltpu.VMEM((half, width), F32),
            pltpu.SemaphoreType.DMA((9,)),
        ],
        out_specs=(HBM, HBM),
        flops=6 * width**3,
        nbytes=16 * width**2,
        limit=60,
    )(live_cols, right, inverse, coupling)
    top_inverse, a0 = lax.optimization_barrier((top_inverse, a0))
    blocks = lax.all_gather(top_inverse, "ga", axis_index_groups=y_groups)
    a3 = ring(a0, 1)
    b1 = ring(b0, -1)
    b3 = ring(b0, 1)
    a1 = ring(a0, -1)
    a2 = ring(a3, 1)
    b2 = ring(b1, -1)

    staged = kernel_call(
        stage,
        pair(ROW - 1, width, width) + (shape(ROW - 1, rhs, width),),
        [VMEM] * 6,
        nbytes=32 * width**2,
    )(a0, b0, a1, b1, a3, b3)
    nh, nl, group, last = kernel_call(
        assemble,
        pair(ROW, width, width) + (shape(ROW, rhs, width), shape(rhs, width)),
        [VMEM] * 5,
        flops=24 * rhs * width**2,
        nbytes=32 * width**2,
    )(*staged, a2, b2)
    came = [hop(last, 0, 1)]
    products, store = kernel_call(
        multiply_up,
        (shape(4, width, width, kind=BF16), shape(STORE, width, width, kind=BF16)),
        [VMEM, VMEM],
        scratch=[pltpu.SemaphoreType.DMA((2,))],
        out_specs=(VMEM, HBM),
        flops=18 * width**3,
        nbytes=24 * width**2,
    )(nh, nl)
    blocks, came[0], products = lax.optimization_barrier((blocks, came[0], products))
    packed = kernel_call(
        pack_lower,
        shape(top_inverse.shape[0], top * (ga // ROW + 1) // 2),
        [VMEM],
        nbytes=2 * top**2,
    )(blocks)
    for row in range(1, chain_rows - 1):
        moved = kernel_call(
            hop_forward, shape(rhs, width), [VMEM] * 3, flops=6 * rhs * width**2
        )(last, came[-1], products)
        came.append(hop(moved, row, 1))
        if row == 1:
            packed, came[-1] = lax.optimization_barrier((packed, came[-1]))
    packed = lax.all_gather(packed, "ga", axis_index_groups=x_groups)

    tiles = (ga, rhs * top // ga // 128, 128)
    solved, partial = kernel_call(
        contribute,
        (shape(rhs, width), shape(*tiles)),
        [VMEM] * (5 + len(came)),
        flops=12 * rhs * width**2,
    )(group, products, across, rows, top_right, *came)
    partial = lax.all_to_all(partial, "ga", 0, 0)
    partial = kernel_call(total_of, shape(gz, *tiles[1:]), [VMEM])(partial)
    partial = lax.all_to_all(partial, "gz", 0, 0)
    partial = kernel_call(total_of, shape(*tiles), [VMEM])(partial)
    partial = lax.all_to_all(partial, "ga", 0, 0)
    partial, packed = lax.optimization_barrier((partial, packed))
    top_solution, nh, nl = kernel_call(
        solve_top,
        (shape(rhs, top),) + pair(ROW, width, width),
        [VMEM, VMEM, HBM],
        scratch=[
            pltpu.VMEM((top, top), BF16),
            pltpu.VMEM((top, top), BF16),
            pltpu.SemaphoreType.DMA((2,)),
        ],
        flops=12 * rhs * top**2,
    )(partial, packed, store)
    reduced = kernel_call(
        lift, shape(ROW, rhs, width), [VMEM] * 4, flops=6 * rhs * top * width
    )(top_solution, across, rows, solved)

    reduced = lax.all_to_all(reduced, "ga", 0, 0, axis_index_groups=x_groups)
    own, sent = kernel_call(
        row_backward,
        (shape(rhs, width), shape(rhs, width)),
        [VMEM] * 3,
        flops=24 * rhs * width**2,
    )(reduced, nh, nl)
    came = [hop(sent, chain_rows - 1, -1)]
    settled, zh, zl = kernel_call(
        tail,
        (shape(rhs, width),) + pair(width, width),
        [SMEM] + [VMEM] * 4,
        flops=18 * width**3,
        nbytes=24 * width**2,
    )(live_cols, own, nh, nl, inverse)
    for row in range(chain_rows - 2, 0, -1):
        moved = kernel_call(
            hop_backward, shape(rhs, width), [VMEM] * 3, flops=6 * rhs * width**2
        )(sent, came[-1], products)
        came.append(hop(moved, row, -1))
    result = kernel_call(
        finish, shape(rhs, width), [VMEM] * (3 + len(came)), flops=6 * rhs * width**2
    )(settled, zh, zl, *came)
    return (result[None, None], top_solution)


def solution(mesh):
    placed = (
        P("gz", "ga", None, None),
        P("gz", "ga", None, None),
        P("gz", "ga", None, None),
        P("gz", "ga", None, None),
        P("gz", "ga", None),
        P("gz", "ga"),
        P(),
        P("ga", None),
    )
    return jax.shard_map(
        shards,
        mesh=mesh,
        in_specs=placed,
        out_specs=(P("gz", "ga", None, None), P()),
        check_vma=False,
    )
```
